512 devices in a mesh: dp: 32 (over z, y_lo), seq: 16 (over y_hi, x, core).
Axes of the slice: x: 4, y: 4 (y_hi: 2, y_lo: 2; y = y_hi * 2 + y_lo), z: 16, core: 2. Of those that a mesh axis runs over, the one named last changes fastest.
Arguments:
- normed_layer_input: bfloat16 [32, 2560, 4096], P('dp', 'seq'), may hold values from -6 to 6
- queries: bfloat16 [32, 2560, 2048], P('dp', 'seq'), may hold values from -8 to 8
- keys: bfloat16 [32, 2560, 2048], P('dp', 'seq'), may hold values from -8 to 8
- values: bfloat16 [32, 2560, 2048], P('dp', 'seq'), may hold values from -6 to 6
- output_gradient: bfloat16 [32, 2560, 2048], P('dp', 'seq'), may hold values from -0.59765625 to 0.59765625
- adapter_down_weight: bfloat16 [4096, 96], replicated, may hold values from -0.09375 to 0.09375
- adapter_up_weight: bfloat16 [32, 6144], replicated, may hold values from -1 to 1
- head_order: int32 [16], replicated, may hold values from 0 to 15, each once
Outputs:
- lora_down_grad: bfloat16 [4096, 96], P(('dp', 'seq'))
- lora_up_grad: bfloat16 [32, 6144], P(None, ('dp', 'seq'))
The draws below stay inside these ranges and needn't reach their ends.
Inputs may be any that keep to these rules, and one draw needn't show every extreme that they name: `head_order`: every head number appears exactly once.
All inputs are finite; a program needn't handle non-finite values.
Results may differ from the reference program's by a relative error of at most 0.017.
Values may be sent and summed in bfloat16 or wider, within the bound.
No kernel may reach another device: no remote copies, remote signals or barrier semaphores. Data moves between devices by JAX's collectives and lax.ppermute only.
A program may use at most 64 MiB of HBM per device.

```python
import jax
import jax.numpy as jnp
from jax import lax

MODEL_WIDTH = 4096
HEAD_TOTAL = 16
HEAD_SIZE = 128
ADAPTER_RANK = 32
GROUP = 160
HALF = 80
L = 2560
SEQS = 32


def draw_queries(key, part):
    key = jax.random.fold_in(key, 11)
    array_extent = (SEQS, L, HEAD_TOTAL * HEAD_SIZE)
    return jnp.clip(jax.random.normal(key, array_extent, jnp.float32), -8.0, 8.0).astype(jnp.bfloat16)


def draw_keys(key, part):
    key = jax.random.fold_in(key, 13)
    array_extent = (SEQS, L, HEAD_TOTAL * HEAD_SIZE)
    return jnp.clip(jax.random.normal(key, array_extent, jnp.float32), -8.0, 8.0).astype(jnp.bfloat16)


def block_levels(stream_key, extent, split, low, top_value):
    def one(dim, shards_of):
        heights = jax.random.uniform(jax.random.fold_in(jax.random.fold_in(stream_key, 6), dim), (shards_of,), jnp.float32, low / len(split), top_value / len(split))
        return jnp.repeat(jnp.exp(heights), extent[dim] // shards_of).reshape((-1,) + (1,) * (len(extent) - dim - 1))

    level = one(*split[0])
    for cut in split[1:]:
        level = level * one(*cut)
    return level


def noise(own_key, shape, spread, reach, shards=(), kind=jnp.bfloat16):
    gain = block_levels(own_key, shape, shards, -0.22, 0.18) if shards else 1.0
    values = jax.random.normal(own_key, shape, jnp.float32) * spread * gain
    return jnp.minimum(jnp.maximum(values, -reach), reach).astype(kind)


def setup_inputs(seed: int = 0) -> dict:
    streams_of = jax.random.split(jax.random.key(seed), 9)
    normed_layer_input = noise(streams_of[0], (SEQS, L, MODEL_WIDTH), 1.0, 6.0, ((0, 32), (1, 16)))
    queries = draw_queries(jax.random.fold_in(streams_of[8], 71), 0)
    keys = draw_keys(jax.random.fold_in(streams_of[8], 71), 0)
    values = noise(streams_of[3], (SEQS, L, HEAD_TOTAL * HEAD_SIZE), 1.0, 6.0, ((0, 32), (1, 16)))
    output_gradient = noise(streams_of[4], (SEQS, L, HEAD_TOTAL * HEAD_SIZE), 0.1, 0.59765625, ((0, 32), (1, 16)))
    adapter_down_weight = noise(streams_of[5], (MODEL_WIDTH, 3 * ADAPTER_RANK), MODEL_WIDTH ** -0.5, 0.09375)
    adapter_up_weight = noise(streams_of[6], (ADAPTER_RANK, 3 * HEAD_TOTAL * HEAD_SIZE), ADAPTER_RANK ** -0.5, 1.0)
    head_order = jax.random.permutation(streams_of[7], HEAD_TOTAL).astype(jnp.int32)
    return {"normed_layer_input": normed_layer_input, "queries": queries, "keys": keys, "values": values, "output_gradient": output_gradient, "adapter_down_weight": adapter_down_weight, "adapter_up_weight": adapter_up_weight, "head_order": head_order}


ADAPTER_SCALE = 0.25


def attend(query, key_in, value, cotangent):
    qf = query.astype(jnp.float32)
    kf = key_in.astype(jnp.float32)
    vf = value.astype(jnp.float32)
    df = cotangent.astype(jnp.float32)
    scale = HEAD_SIZE ** -0.5
    size = query.shape[1]
    causal = jnp.arange(size)[:, None] >= jnp.arange(size)[None, :]
    scores = jnp.einsum('gqhd,gkhd->ghqk', qf, kf) * scale
    scores = jnp.where(causal, scores, -jnp.inf)
    probs = jax.nn.softmax(scores, axis=-1)
    weights = lax.optimization_barrier(probs.astype(jnp.bfloat16)).astype(jnp.float32)
    output = jnp.einsum('ghqk,gkhd->gqhd', weights, vf)
    delta = jnp.sum(df * output, axis=-1)
    delta = jnp.moveaxis(delta, 2, 1)[..., None]
    dvalue = jnp.einsum('ghqk,gqhd->gkhd', weights, df).astype(jnp.bfloat16)
    dprob = jnp.einsum('gqhd,gkhd->ghqk', df, vf)
    dscore = lax.optimization_barrier((probs * (dprob - delta)).astype(jnp.bfloat16)).astype(jnp.float32)
    dquery = (jnp.einsum('ghqk,gkhd->gqhd', dscore, kf) * scale).astype(jnp.bfloat16)
    dkey = (jnp.einsum('ghqk,gqhd->gkhd', dscore, qf) * scale).astype(jnp.bfloat16)
    return dquery, dkey, dvalue


def pick(array, head_ids, rolled):
    chosen = jnp.take(array, head_ids, axis=1)
    if rolled:
        chosen = jnp.roll(chosen, -HALF, axis=0)
    return chosen.reshape(L // GROUP, GROUP, chosen.shape[1], HEAD_SIZE)


def unpick(array, rolled):
    flat = array.reshape(L, array.shape[2], HEAD_SIZE)
    if rolled:
        flat = jnp.roll(flat, HALF, axis=0)
    return flat


def reference(normed_layer_input, queries, keys, values, output_gradient, adapter_down_weight, adapter_up_weight, head_order):
    output_width = HEAD_TOTAL * HEAD_SIZE
    rotated_ids = head_order[:HEAD_TOTAL // 2]
    unmoved_ids = head_order[HEAD_TOTAL // 2:]

    def one_sequence(carry, items):
        input_arrays, qseq, kseq, vseq, dseq = items
        array_extent = (L, HEAD_TOTAL, HEAD_SIZE)
        arrays = [qseq.reshape(array_extent), kseq.reshape(array_extent), vseq.reshape(array_extent), dseq.reshape(array_extent)]
        grads = [jnp.zeros(array_extent, jnp.bfloat16) for index_g in range(3)]
        for head_ids, rolled in ((unmoved_ids, False), (rotated_ids, True)):
            parts = attend(*[pick(item, head_ids, rolled) for item in arrays])
            grads = [full.at[:, head_ids].set(unpick(part, rolled)) for full, part in zip(grads, parts)]
        stacked_weight = jnp.concatenate([item.reshape(L, output_width) for item in grads], axis=1)
        reduced_rank_term = jnp.dot(input_arrays, adapter_down_weight, preferred_element_type=jnp.float32).astype(jnp.bfloat16)
        projection_kind = jnp.concatenate([jnp.dot(stacked_weight[:, projection_index * output_width:(projection_index + 1) * output_width], adapter_up_weight[:, projection_index * output_width:(projection_index + 1) * output_width].T, preferred_element_type=jnp.float32) for projection_index in range(3)], axis=1).astype(jnp.bfloat16)
        down_projection_sum = carry[0] + jnp.dot(input_arrays.T, projection_kind, preferred_element_type=jnp.float32)
        up_projection_sum = carry[1] + jnp.concatenate([jnp.dot(reduced_rank_term[:, projection_index * ADAPTER_RANK:(projection_index + 1) * ADAPTER_RANK].T, stacked_weight[:, projection_index * output_width:(projection_index + 1) * output_width], preferred_element_type=jnp.float32) for projection_index in range(3)], axis=1)
        return (down_projection_sum, up_projection_sum), None

    start = (jnp.zeros((MODEL_WIDTH, 3 * ADAPTER_RANK), jnp.float32), jnp.zeros((ADAPTER_RANK, 3 * output_width), jnp.float32))
    (down_projection_sum, up_projection_sum), unused = lax.scan(one_sequence, start, (normed_layer_input, queries, keys, values, output_gradient))
    return (ADAPTER_SCALE * down_projection_sum).astype(jnp.bfloat16), (ADAPTER_SCALE * up_projection_sum).astype(jnp.bfloat16)
```

```python
import jax
import jax.numpy as jnp
from jax import lax
from jax.experimental import pallas as pl
from jax.experimental.pallas import tpu as pltpu
from jax.sharding import Mesh
from jax.sharding import PartitionSpec as P

HEAD = 128
ROWS = 160
HALF = 80
HEADS = 16
SHIFTED = 8
WIDTH = HEADS * HEAD
MODEL = 4096
RANK = 32
SCALE = HEAD ** -0.5
ADAPTER_SCALE = 0.25
Z, G, C = 16, 16, 2
PART = Z * 8 + 16

BF16, F32 = jnp.bfloat16, jnp.float32
VMEM = pl.BlockSpec(memory_space=pltpu.VMEM)
SMEM = pl.BlockSpec(memory_space=pltpu.SMEM)


def call(body, name, out_shape, in_specs, flops, size, limit=32, **rest):
    return pl.pallas_call(
        body,
        name=name,
        out_shape=out_shape,
        in_specs=in_specs,
        out_specs=jax.tree.map(lambda _: VMEM, out_shape),
        compiler_params=pltpu.CompilerParams(vmem_limit_bytes=limit * 1024 * 1024),
        cost_estimate=pl.CostEstimate(flops=flops, bytes_accessed=size, transcendentals=0),
        **rest,
    )


def dot(left, right):
    return jnp.dot(left, right, preferred_element_type=F32)


def dot_last(left, right):
    return lax.dot_general(left, right, (((1,), (1,)), ((), ())), preferred_element_type=F32)


def dot_first(left, right):
    return lax.dot_general(left, right, (((0,), (0,)), ((), ())), preferred_element_type=F32)


def attend(query, key, value, cotangent, allowed):
    scores = jnp.where(allowed, dot_last(key, query), -jnp.inf)
    top = jnp.max(scores, axis=0, keepdims=True)
    powers = jnp.exp((scores - top) * SCALE)
    probs = powers / jnp.sum(powers, axis=0, keepdims=True)
    weights = probs.astype(BF16)
    dprob = dot_last(value, cotangent)
    delta = jnp.sum(weights.astype(F32) * dprob, axis=0, keepdims=True)
    dscore = (probs * (dprob - delta)).astype(BF16)
    dquery = (dot_first(dscore, key) * SCALE).astype(BF16)
    dkey = (dot(dscore, query) * SCALE).astype(BF16)
    dvalue = dot(weights, cotangent).astype(BF16)
    return dquery, dkey, dvalue


def causal(keys, queries, ahead):
    row = lax.broadcasted_iota(jnp.int32, (keys, queries), 0)
    column = lax.broadcasted_iota(jnp.int32, (keys, queries), 1)
    return row <= column + ahead


def lanes_of(order_ref, slot, block=0):
    return pl.ds(pl.multiple_of(order_ref[slot] * HEAD + block * WIDTH, HEAD), HEAD)


def first_kernel(order_ref, normed_ref, down_ref, key_ref, value_ref, send_ref, low_ref):
    low = dot(normed_ref[...], down_ref[...]).astype(BF16)
    low = jnp.concatenate([low, jnp.zeros((ROWS, HEAD - 3 * RANK), BF16)], axis=1)
    low_ref[...] = low
    send_ref[:, 2 * SHIFTED * HEAD :] = low[HALF:]
    for slot in range(SHIFTED):
        lanes = lanes_of(order_ref, slot)
        send_ref[:, slot * HEAD : (slot + 1) * HEAD] = key_ref[HALF:, lanes]
        send_ref[:, (SHIFTED + slot) * HEAD : (SHIFTED + slot + 1) * HEAD] = value_ref[HALF:, lanes]


def own_kernel(order_ref, query_ref, key_ref, value_ref, cot_ref, out_ref):
    whole = causal(ROWS, ROWS, 0)
    half = causal(HALF, HALF, 0)
    nothing = jnp.zeros((HALF, HEAD), BF16)
    for slot in range(SHIFTED, HEADS):
        lanes = lanes_of(order_ref, slot)
        grads = attend(query_ref[:, lanes], key_ref[:, lanes], value_ref[:, lanes], cot_ref[:, lanes], whole)
        for block in range(3):
            out_ref[:ROWS, lanes_of(order_ref, slot, block)] = grads[block]
            out_ref[ROWS:, lanes_of(order_ref, slot, block)] = nothing
    for slot in range(SHIFTED):
        lanes = lanes_of(order_ref, slot)
        grads = attend(
            query_ref[HALF:, lanes], key_ref[HALF:, lanes], value_ref[HALF:, lanes], cot_ref[HALF:, lanes], half
        )
        for block in range(3):
            out_ref[HALF:ROWS, lanes_of(order_ref, slot, block)] = grads[block]


def joint_kernel(
    order_ref, query_ref, key_ref, value_ref, cot_ref, come_ref, up_ref, have_ref, out_ref, proj_ref, back_ref
):
    out_ref[...] = have_ref[...]
    allowed = causal(ROWS, HALF, HALF)
    nothing = jnp.zeros((HALF, HEAD), BF16)
    for slot in range(SHIFTED):
        lanes = lanes_of(order_ref, slot)
        far_key = come_ref[:, slot * HEAD : (slot + 1) * HEAD]
        far_value = come_ref[:, (SHIFTED + slot) * HEAD : (SHIFTED + slot + 1) * HEAD]
        key = jnp.concatenate([far_key, key_ref[:HALF, lanes]], axis=0)
        value = jnp.concatenate([far_value, value_ref[:HALF, lanes]], axis=0)
        dquery, dkey, dvalue = attend(query_ref[:HALF, lanes], key, value, cot_ref[:HALF, lanes], allowed)
        out_ref[:HALF, lanes] = dquery
        out_ref[ROWS:, lanes] = nothing
        for block, grad in ((1, dkey), (2, dvalue)):
            out_ref[:HALF, lanes_of(order_ref, slot, block)] = grad[HALF:]
            out_ref[ROWS:, lanes_of(order_ref, slot, block)] = grad[:HALF]
    total = jnp.zeros((ROWS + HALF, HEAD), F32)
    for block in range(3):
        columns = slice(block * WIDTH, (block + 1) * WIDTH)
        parts = [up_ref[:, columns] if place == block else jnp.zeros((RANK, WIDTH), BF16) for place in range(4)]
        total = total + dot_last(out_ref[:, columns], jnp.concatenate(parts, axis=0))
    proj_ref[...] = total[:ROWS]
    back_ref[...] = total[ROWS:]


def up_kernel(grads_ref, low_ref, come_ref, out_ref, sums_ref):
    low = jnp.concatenate([low_ref[...], come_ref[...]], axis=0).astype(F32)
    lane = lax.broadcasted_iota(jnp.int32, low.shape, 1) // RANK
    span = WIDTH // 4
    for chunk in range(12):
        block, quarter = chunk // 4, chunk // 3
        right = jnp.zeros_like(low)
        for place in sorted({quarter, 3}):
            turned = pltpu.roll(low, (place - block) % 4 * RANK, 1) if place != block else low
            right = jnp.where(lane == place, turned, right)
        sums_ref[chunk * span : (chunk + 1) * span, :] = dot_first(
            grads_ref[:, chunk * span : (chunk + 1) * span], right.astype(BF16)
        )
    place = lax.broadcasted_iota(jnp.int32, (8, HEAD), 1) // RANK
    upper = lax.broadcasted_iota(jnp.int32, (8, HEAD), 0) < 4

    def tile(z, g, third):
        start = ((z * G + g) * 3 + third) * 8
        return sums_ref[start : start + 8, :]

    for g in range(G):
        for z in range(0, Z, 2):
            for c in range(C):
                pair = jnp.concatenate([tile(z, g, 2 * c), tile(z + 1, g, 2 * c)], axis=0)
                out_ref[c, g, z * 8 : z * 8 + 16, :] = pair.astype(BF16)
        middle = []
        for low_z in range(4):
            merged = tile(low_z, g, 1)
            for quarter in range(1, 4):
                merged = jnp.where(place == quarter, tile(4 * quarter + low_z, g, 1), merged)
            middle.append(merged)
        swapped = [pltpu.roll(item, 4, 0) for item in middle]
        for c in range(C):
            rows = []
            for even in (0, 2):
                if c == 0:
                    rows.append(jnp.where(upper, middle[even], swapped[even + 1]))
                else:
                    rows.append(jnp.where(upper, swapped[even], middle[even + 1]))
            out_ref[c, g, Z * 8 :, :] = jnp.concatenate(rows, axis=0).astype(BF16)


def down_kernel(core_ref, normed_ref, proj_ref, back_ref, up_ref, mine_ref, other_ref):
    own = core_ref[0]
    total = proj_ref[...]
    total = jnp.concatenate([total[:HALF], total[HALF:] + back_ref[...]], axis=0).astype(BF16)
    lane = lax.broadcasted_iota(jnp.int32, (16, HEAD), 1)
    for z in range(0, Z, 2):
        part = dot_first(normed_ref[:, z * 256 : (z + 2) * 256], total)
        part = part.reshape(2, G, C, 8, HEAD)
        for g in range(G):
            pieces = []
            for c in range(C):
                down = jnp.concatenate([part[0, g, c], part[1, g, c]], axis=0)
                up = up_ref[c, g, z * 8 : z * 8 + 16, :]
                pieces.append(jnp.where(lane < 3 * RANK, down, up.astype(F32)).astype(BF16))
            start = g * PART + z * 8
            mine_ref[start : start + 16, :] = jnp.where(own == 0, pieces[0], pieces[1])
            other_ref[start : start + 16, :] = jnp.where(own == 0, pieces[1], pieces[0])
    for g in range(G):
        start = g * PART + Z * 8
        pieces = [up_ref[c, g, Z * 8 :, :] for c in range(C)]
        mine_ref[start : start + 16, :] = jnp.where(own == 0, pieces[0], pieces[1])
        other_ref[start : start + 16, :] = jnp.where(own == 0, pieces[1], pieces[0])


def middle_kernel(come_ref, out_ref):
    total = come_ref[0].astype(F32)
    for item in range(1, G):
        total = total + come_ref[item].astype(F32)
    for z in range(Z):
        start = Z * 8 + z % 4 // 2 * 8
        tiles = jnp.concatenate([total[z * 8 : z * 8 + 8], total[start : start + 8]], axis=0)
        out_ref[z] = tiles.astype(BF16)


def last_kernel(place_ref, come_ref, down_ref, up_ref):
    z, c = place_ref[0], place_ref[1]
    total = come_ref[0].astype(F32)
    for item in range(1, Z):
        total = total + come_ref[item].astype(F32)
    total = total * ADAPTER_SCALE
    upper, lower = total[:8], total[8:]
    down_ref[...] = upper[:, : 3 * RANK].astype(BF16)
    lower = pltpu.roll(lower, lax.rem((3 - z // 4) * RANK, HEAD), 1)
    moved = lax.rem(z, 2) != c
    lower = jnp.where(moved, pltpu.roll(lower, 4, 0), lower)
    both = jnp.concatenate([upper, lower], axis=0)
    both = jnp.where(c == 1, pltpu.roll(both, 4, 0), both)
    square = jnp.concatenate([both, jnp.zeros((HEAD - 16, HEAD), F32)], axis=0)
    up_ref[...] = square.T[3 * RANK :, :12].astype(BF16)


def shape(dims, kind=BF16):
    return jax.ShapeDtypeStruct(dims, kind)


def first_call(order, normed, down, keys, values):
    return call(
        first_kernel,
        "send_parts",
        (shape((HALF, (2 * SHIFTED + 1) * HEAD)), shape((ROWS, HEAD))),
        [SMEM, VMEM, VMEM, VMEM, VMEM],
        130_000_000,
        4_000_000,
    )(order, normed, down, keys, values)


def own_call(order, queries, keys, values, cotangent):
    return call(
        own_kernel,
        "own_attention",
        shape((ROWS + HALF, 3 * WIDTH)),
        [SMEM, VMEM, VMEM, VMEM, VMEM],
        2_000_000_000,
        6_000_000,
    )(order, queries, keys, values, cotangent)


def joint_call(order, queries, keys, values, cotangent, come, up, have):
    return call(
        joint_kernel,
        "joint_attention",
        (shape((ROWS + HALF, 3 * WIDTH)), shape((ROWS, HEAD), F32), shape((HALF, HEAD), F32)),
        [SMEM] + [VMEM] * 7,
        1_000_000_000,
        6_000_000,
    )(order, queries, keys, values, cotangent, come, up, have)


def up_call(grads, low, far_low):
    return call(
        up_kernel,
        "up_gradient",
        shape((C, G, PART, HEAD)),
        [VMEM] * 3,
        1_000_000_000,
        6_000_000,
        scratch_shapes=[pltpu.VMEM((3 * WIDTH, HEAD), F32)],
    )(grads, low, far_low)


def down_call(core, normed, proj, back, up):
    return call(
        down_kernel,
        "down_gradient",
        (shape((G * PART, HEAD)), shape((G * PART, HEAD))),
        [SMEM] + [VMEM] * 4,
        500_000_000,
        4_000_000,
    )(core, normed, proj, back, up)


def middle_call(come):
    return call(middle_kernel, "middle_sum", shape((Z, 16, HEAD)), [VMEM], 1_000_000, 600_000)(come)


def last_call(place, come):
    return call(
        last_kernel, "last_sum", (shape((8, 3 * RANK)), shape((RANK, 12))), [SMEM, VMEM], 100_000, 70_000
    )(place, come)


def per_device(normed, queries, keys, values, cotangent, down, up, order):
    normed, queries, keys, values, cotangent = (
        item[0] for item in (normed, queries, keys, values, cotangent)
    )
    z, core = lax.axis_index("z"), lax.axis_index("c")
    ring = ("yh", "x", "c")
    count = 16
    send, low = first_call(order, normed, down, keys, values)
    come = lax.ppermute(send, ring, [(item, (item + 1) % count) for item in range(count)])
    have = own_call(order, queries, keys, values, cotangent)
    grads, proj, back = joint_call(order, queries, keys, values, cotangent, come, up, have)
    back = lax.ppermute(back, ring, [(item, (item - 1) % count) for item in range(count)])
    up_part = up_call(grads, low, come[:, 2 * SHIFTED * HEAD :])
    mine, other = down_call(core.reshape(1), normed, proj, back, up_part)
    other = lax.ppermute(other, "c", [(0, 1), (1, 0)])
    chip = (mine.astype(F32) + other.astype(F32)).astype(BF16)
    plane = lax.all_to_all(chip.reshape(G, PART, HEAD), ("yl", "yh", "x"), 0, 0)
    line = lax.all_to_all(middle_call(plane), "z", 0, 0)
    return last_call(jnp.stack([z, core]), line)


def solution(mesh):
    fine = Mesh(mesh.devices.reshape(Z, 2, 2, 4, C), ("z", "yl", "yh", "x", "c"))
    dp, seq = ("z", "yl"), ("yh", "x", "c")
    tokens = P(dp, seq, None)
    in_specs = (tokens,) * 5 + (P(),) * 3
    out_specs = (P(dp + seq, None), P(None, dp + seq))
    return jax.shard_map(per_device, mesh=fine, in_specs=in_specs, out_specs=out_specs, check_vma=False)
```

```python
import jax
import jax.numpy as jnp
from jax import lax
from jax.experimental import pallas as pl
from jax.experimental.pallas import tpu as pltpu
from jax.sharding import Mesh
from jax.sharding import PartitionSpec as P

HEAD = 128
ROWS = 160
HALF = 80
HEADS = 16
SHIFTED = 8
WIDTH = HEADS * HEAD
MODEL = 4096
RANK = 32
SCALE = HEAD ** -0.5
ADAPTER_SCALE = 0.25
NEAR, FAR = ("yl", "yh", "x"), ("z",)
Z, G, C = 16, 16, 2
BAND = Z // 4
WIDE = 4
PART = Z * 8 + BAND * 4

BF16, F32 = jnp.bfloat16, jnp.float32
VMEM = pl.BlockSpec(memory_space=pltpu.VMEM)
SMEM = pl.BlockSpec(memory_space=pltpu.SMEM)
HBM = pl.BlockSpec(memory_space=pltpu.HBM)


def call(body, name, out_shape, in_specs, flops, size, limit=32, **rest):
    return pl.pallas_call(
        body,
        name=name,
        out_shape=out_shape,
        in_specs=in_specs,
        out_specs=jax.tree.map(lambda _: VMEM, out_shape),
        compiler_params=pltpu.CompilerParams(vmem_limit_bytes=limit * 1024 * 1024),
        cost_estimate=pl.CostEstimate(flops=flops, bytes_accessed=size, transcendentals=0),
        **rest,
    )


def dot(left, right):
    return jnp.dot(left, right, preferred_element_type=F32)


def dot_last(left, right):
    return lax.dot_general(left, right, (((1,), (1,)), ((), ())), preferred_element_type=F32)


def dot_first(left, right):
    return lax.dot_general(left, right, (((0,), (0,)), ((), ())), preferred_element_type=F32)


def attend(query, key, value, cotangent, allowed):
    scores = jnp.where(allowed, dot_last(key, query), -jnp.inf)
    top = jnp.max(scores, axis=0, keepdims=True)
    powers = jnp.exp((scores - top) * SCALE)
    probs = powers / jnp.sum(powers, axis=0, keepdims=True)
    weights = probs.astype(BF16)
    dprob = dot_last(value, cotangent)
    delta = jnp.sum(weights.astype(F32) * dprob, axis=0, keepdims=True)
    dscore = (probs * (dprob - delta)).astype(BF16)
    dquery = (dot_first(dscore, key) * SCALE).astype(BF16)
    dkey = (dot(dscore, query) * SCALE).astype(BF16)
    dvalue = dot(weights, cotangent).astype(BF16)
    return dquery, dkey, dvalue


def causal(keys, queries, ahead):
    row = lax.broadcasted_iota(jnp.int32, (keys, queries), 0)
    column = lax.broadcasted_iota(jnp.int32, (keys, queries), 1)
    return row <= column + ahead


def lanes_of(order_ref, slot, block=0):
    return pl.ds(pl.multiple_of(order_ref[slot] * HEAD + block * WIDTH, HEAD), HEAD)


def first_kernel(
    order_ref, key_ref, value_ref, normed_ref, down_ref, send_ref, low_ref, normed_own, down_own, sems, wide_sems
):
    copies, wide_copies = [], []
    span = MODEL // WIDE
    for part in range(WIDE):
        lanes = slice(part * span, (part + 1) * span)
        for item, (source, target) in enumerate(((normed_ref, normed_own), (down_ref, down_own))):
            copy = pltpu.make_async_copy(source.at[:, lanes], target.at[:, lanes], wide_sems.at[item, part])
            copy.start()
            wide_copies.append(copy)
    for place in range(2 * SHIFTED):
        copy = pltpu.make_async_copy(
            (key_ref if place < SHIFTED else value_ref).at[HALF:, lanes_of(order_ref, place % SHIFTED)],
            send_ref.at[:, place * HEAD : (place + 1) * HEAD],
            sems.at[place],
        )
        copy.start()
        copies.append(copy)
    for copy in wide_copies:
        copy.wait()
    low = dot_last(normed_own[...], down_own[...]).astype(BF16)
    low = jnp.concatenate([low, jnp.zeros((ROWS, HEAD - 3 * RANK), BF16)], axis=1)
    low_ref[...] = low
    send_ref[:, 2 * SHIFTED * HEAD :] = low[HALF:]
    for copy in copies:
        copy.wait()


def own_kernel(order_ref, query_ref, key_ref, value_ref, cot_ref, out_ref):
    whole = causal(ROWS, ROWS, 0)
    half = causal(HALF, HALF, 0)
    nothing = jnp.zeros((HALF, HEAD), BF16)
    for slot in range(SHIFTED, HEADS):
        lanes = lanes_of(order_ref, slot)
        grads = attend(query_ref[:, lanes], key_ref[:, lanes], value_ref[:, lanes], cot_ref[:, lanes], whole)
        for block in range(3):
            out_ref[:ROWS, lanes_of(order_ref, slot, block)] = grads[block]
            out_ref[ROWS:, lanes_of(order_ref, slot, block)] = nothing
    for slot in range(SHIFTED):
        lanes = lanes_of(order_ref, slot)
        grads = attend(
            query_ref[HALF:, lanes], key_ref[HALF:, lanes], value_ref[HALF:, lanes], cot_ref[HALF:, lanes], half
        )
        for block in range(3):
            out_ref[HALF:ROWS, lanes_of(order_ref, slot, block)] = grads[block]


def joint_kernel(
    order_ref, query_ref, key_ref, value_ref, cot_ref, come_ref, up_ref, have_ref, out_ref, proj_ref, back_ref
):
    del have_ref
    allowed = causal(ROWS, HALF, HALF)
    nothing = jnp.zeros((HALF, HEAD), BF16)
    for slot in range(SHIFTED):
        lanes = lanes_of(order_ref, slot)
        far_key = come_ref[:, slot * HEAD : (slot + 1) * HEAD]
        far_value = come_ref[:, (SHIFTED + slot) * HEAD : (SHIFTED + slot + 1) * HEAD]
        key = jnp.concatenate([far_key, key_ref[:HALF, lanes]], axis=0)
        value = jnp.concatenate([far_value, value_ref[:HALF, lanes]], axis=0)
        dquery, dkey, dvalue = attend(query_ref[:HALF, lanes], key, value, cot_ref[:HALF, lanes], allowed)
        out_ref[:HALF, lanes] = dquery
        out_ref[ROWS:, lanes] = nothing
        for block, grad in ((1, dkey), (2, dvalue)):
            out_ref[:HALF, lanes_of(order_ref, slot, block)] = grad[HALF:]
            out_ref[ROWS:, lanes_of(order_ref, slot, block)] = grad[:HALF]
    total = jnp.zeros((ROWS + HALF, HEAD), F32)
    for block in range(3):
        columns = slice(block * WIDTH, (block + 1) * WIDTH)
        parts = [up_ref[:, columns] if place == block else jnp.zeros((RANK, WIDTH), BF16) for place in range(4)]
        total = total + dot_last(out_ref[:, columns], jnp.concatenate(parts, axis=0))
    proj_ref[...] = total[:ROWS]
    back_ref[...] = total[ROWS:]


def up_kernel(grads_ref, low_ref, come_ref, out_ref, sums_ref):
    low = jnp.concatenate([low_ref[...], come_ref[:, 2 * SHIFTED * HEAD :]], axis=0).astype(F32)
    lane = lax.broadcasted_iota(jnp.int32, low.shape, 1) // RANK
    span = WIDTH // 4
    for chunk in range(12):
        block, quarter = chunk // 4, chunk // 3
        right = jnp.zeros_like(low)
        for place in sorted({quarter, 3}):
            turned = pltpu.roll(low, (place - block) % 4 * RANK, 1) if place != block else low
            right = jnp.where(lane == place, turned, right)
        sums_ref[chunk * span : (chunk + 1) * span, :] = dot_first(
            grads_ref[:, chunk * span : (chunk + 1) * span], right.astype(BF16)
        )
    place = lax.broadcasted_iota(jnp.int32, (8, HEAD), 1) // RANK
    upper = lax.broadcasted_iota(jnp.int32, (8, HEAD), 0) < 4

    def tile(z, g, third):
        start = ((z * G + g) * 3 + third) * 8
        return sums_ref[start : start + 8, :]

    for g in range(G):
        for z in range(0, Z, 2):
            for c in range(C):
                pair = jnp.concatenate([tile(z, g, 2 * c), tile(z + 1, g, 2 * c)], axis=0)
                out_ref[c, g, z * 8 : z * 8 + 16, :] = pair.astype(BF16)
        middle = []
        for low_z in range(BAND):
            merged = tile(low_z, g, 1)
            for quarter in range(1, 4):
                merged = jnp.where(place == quarter, tile(BAND * quarter + low_z, g, 1), merged)
            middle.append(merged)
        swapped = [pltpu.roll(item, 4, 0) for item in middle]
        for c in range(C):
            rows = []
            for even in range(0, BAND, 2):
                if c == 0:
                    rows.append(jnp.where(upper, middle[even], swapped[even + 1]))
                else:
                    rows.append(jnp.where(upper, swapped[even], middle[even + 1]))
            out_ref[c, g, Z * 8 :, :] = jnp.concatenate(rows, axis=0).astype(BF16)


def down_kernel(core_ref, normed_ref, proj_ref, back_ref, up_ref, mine_ref, other_ref):
    own = core_ref[0]
    total = proj_ref[...]
    total = jnp.concatenate([total[:HALF], total[HALF:] + back_ref[...]], axis=0).astype(BF16)
    lane = lax.broadcasted_iota(jnp.int32, (16, HEAD), 1)
    for z in range(0, Z, 2):
        part = dot_first(normed_ref[:, z * G * 16 : (z + 2) * G * 16], total)
        part = part.reshape(2, G, C, 8, HEAD)
        for g in range(G):
            pieces = []
            for c in range(C):
                down = jnp.concatenate([part[0, g, c], part[1, g, c]], axis=0)
                up = up_ref[c, g, z * 8 : z * 8 + 16, :]
                pieces.append(jnp.where(lane < 3 * RANK, down, up.astype(F32)).astype(BF16))
            start = g * PART + z * 8
            mine_ref[start : start + 16, :] = jnp.where(own == 0, pieces[0], pieces[1])
            other_ref[start : start + 16, :] = jnp.where(own == 0, pieces[1], pieces[0])
    for g in range(G):
        span = slice(g * PART + Z * 8, (g + 1) * PART)
        pieces = [up_ref[c, g, Z * 8 :, :] for c in range(C)]
        mine_ref[span, :] = jnp.where(own == 0, pieces[0], pieces[1])
        other_ref[span, :] = jnp.where(own == 0, pieces[1], pieces[0])


def middle_kernel(come_ref, out_ref):
    total = come_ref[0].astype(F32)
    for item in range(1, G):
        total = total + come_ref[item].astype(F32)
    for z in range(Z):
        start = Z * 8 + z % BAND // 2 * 8
        tiles = jnp.concatenate([total[z * 8 : z * 8 + 8], total[start : start + 8]], axis=0)
        out_ref[z] = tiles.astype(BF16)


def last_kernel(place_ref, come_ref, down_ref, up_ref):
    z, c = place_ref[0], place_ref[1]
    total = come_ref[0].astype(F32)
    for item in range(1, Z):
        total = total + come_ref[item].astype(F32)
    total = total * ADAPTER_SCALE
    upper, lower = total[:8], total[8:]
    down_ref[...] = upper[:, : 3 * RANK].astype(BF16)
    lower = pltpu.roll(lower, (3 - z // BAND) * RANK, 1)
    moved = lax.rem(z, 2) != c
    lower = jnp.where(moved, pltpu.roll(lower, 4, 0), lower)
    both = jnp.concatenate([upper, lower], axis=0)
    both = jnp.where(c == 1, pltpu.roll(both, 4, 0), both)
    up_ref[...] = both[:12, 3 * RANK :].astype(BF16)


def shape(dims, kind=BF16):
    return jax.ShapeDtypeStruct(dims, kind)


def first_call(order, keys, values, normed, down):
    return call(
        first_kernel,
        "send_parts",
        (shape((HALF, (2 * SHIFTED + 1) * HEAD)), shape((ROWS, HEAD))),
        [SMEM, HBM, HBM, HBM, HBM],
        130_000_000,
        3_000_000,
        limit=63,
        scratch_shapes=[
            pltpu.VMEM(normed.shape, BF16),
            pltpu.VMEM(down.shape, BF16),
            pltpu.SemaphoreType.DMA((2 * SHIFTED,)),
            pltpu.SemaphoreType.DMA((2, WIDE)),
        ],
    )(order, keys, values, normed, down)


def own_call(order, queries, keys, values, cotangent):
    return call(
        own_kernel,
        "own_attention",
        shape((ROWS + HALF, 3 * WIDTH)),
        [SMEM, VMEM, VMEM, VMEM, VMEM],
        2_000_000_000,
        6_000_000,
    )(order, queries, keys, values, cotangent)


def joint_call(order, queries, keys, values, cotangent, come, up, have):
    return call(
        joint_kernel,
        "joint_attention",
        (shape((ROWS + HALF, 3 * WIDTH)), shape((ROWS, HEAD), F32), shape((HALF, HEAD), F32)),
        [SMEM] + [VMEM] * 7,
        1_000_000_000,
        6_000_000,
        input_output_aliases={7: 0},
    )(order, queries, keys, values, cotangent, come, up, have)


def up_call(grads, low, come):
    return call(
        up_kernel,
        "up_gradient",
        shape((C, G, PART, HEAD)),
        [VMEM] * 3,
        1_000_000_000,
        6_000_000,
        scratch_shapes=[pltpu.VMEM((3 * WIDTH, HEAD), F32)],
    )(grads, low, come)


def down_call(core, normed, proj, back, up):
    return call(
        down_kernel,
        "down_gradient",
        (shape((G * PART, HEAD)), shape((G * PART, HEAD))),
        [SMEM] + [VMEM] * 4,
        500_000_000,
        4_000_000,
    )(core, normed, proj, back, up)


def middle_call(come):
    return call(middle_kernel, "middle_sum", shape((Z, 16, HEAD)), [VMEM], 1_000_000, 600_000)(come)


def last_call(place, come):
    return call(
        last_kernel, "last_sum", (shape((8, 3 * RANK)), shape((12, RANK))), [SMEM, VMEM], 100_000, 70_000
    )(place, come)


def per_device(normed, queries, keys, values, cotangent, down, up, order):
    normed, queries, keys, values, cotangent = (
        item[0] for item in (normed, queries, keys, values, cotangent)
    )
    far, core = lax.axis_index(FAR), lax.axis_index("c")
    ring = ("yh", "x", "c")
    count = 16
    ahead = [(item, (item + 1) % count) for item in range(count)]
    behind = [(item, (item - 1) % count) for item in range(count)]
    send, low = first_call(order, keys, values, normed, down.T)
    come = lax.ppermute(send, ring, ahead)
    have = own_call(order, queries, keys, values, cotangent)
    grads, proj, back = joint_call(order, queries, keys, values, cotangent, come, up, have)
    back = lax.ppermute(back, ring, behind)
    up_part = up_call(grads, low, come)
    mine, other = down_call(core.reshape(1), normed, proj, back, up_part)
    other = lax.ppermute(other, "c", [(0, 1), (1, 0)])
    chip = (mine.astype(F32) + other.astype(F32)).astype(BF16)
    plane = lax.all_to_all(chip.reshape(G, PART, HEAD), NEAR, 0, 0)
    line = lax.all_to_all(middle_call(plane), FAR, 0, 0)
    down_grad, up_grad = last_call(jnp.stack([far, core]), line)
    return down_grad, up_grad.T


def solution(mesh):
    fine = Mesh(mesh.devices.reshape(16, 2, 2, 4, 2), ("z", "yl", "yh", "x", "c"))
    dp, seq = ("z", "yl"), ("yh", "x", "c")
    tokens = P(dp, seq, None)
    in_specs = (tokens,) * 5 + (P(),) * 3
    out_specs = (P(dp + seq, None), P(None, dp + seq))
    return jax.shard_map(per_device, mesh=fine, in_specs=in_specs, out_specs=out_specs, check_vma=False)
```

```python
import jax
import jax.numpy as jnp
from jax import lax
from jax.experimental import pallas as pl
from jax.experimental.pallas import tpu as pltpu
from jax.sharding import Mesh
from jax.sharding import PartitionSpec as P

HEAD = 128
ROWS = 160
HALF = 80
HEADS = 16
SHIFTED = 8
WIDTH = HEADS * HEAD
MODEL = 4096
RANK = 32
SCALE = HEAD ** -0.5
ADAPTER_SCALE = 0.25
NEAR, FAR = ("yl", "yh", "x"), ("z",)
Z, G, C = 16, 16, 2
BAND = Z // 4
WIDE = 2
BATCH = 8
PART = Z * 8 + BAND * 4

BF16, F32 = jnp.bfloat16, jnp.float32
VMEM = pl.BlockSpec(memory_space=pltpu.VMEM)
SMEM = pl.BlockSpec(memory_space=pltpu.SMEM)
HBM = pl.BlockSpec(memory_space=pltpu.HBM)


def call(body, name, out_shape, in_specs, flops, size, limit=32, out_specs=None, **rest):
    return pl.pallas_call(
        body,
        name=name,
        out_shape=out_shape,
        in_specs=in_specs,
        out_specs=out_specs or jax.tree.map(lambda _: VMEM, out_shape),
        compiler_params=pltpu.CompilerParams(vmem_limit_bytes=limit * 1024 * 1024),
        cost_estimate=pl.CostEstimate(flops=flops, bytes_accessed=size, transcendentals=0),
        **rest,
    )


def dot(left, right):
    return jnp.dot(left, right, preferred_element_type=F32)


def dot_last(left, right):
    return lax.dot_general(left, right, (((1,), (1,)), ((), ())), preferred_element_type=F32)


def dot_first(left, right):
    return lax.dot_general(left, right, (((0,), (0,)), ((), ())), preferred_element_type=F32)


def attend(parts, allowed):
    queries, keys, values, cotangents = zip(*parts)
    scores = [jnp.where(allowed, dot_last(key, query), -jnp.inf) for query, key in zip(queries, keys)]
    dprobs = [dot_last(value, cotangent) for value, cotangent in zip(values, cotangents)]
    tops = [jnp.max(item, axis=0, keepdims=True) for item in scores]
    powers = [jnp.exp((item - top) * SCALE) for item, top in zip(scores, tops)]
    probs = [item * (1.0 / jnp.sum(item, axis=0, keepdims=True)) for item in powers]
    weights = [item.astype(BF16) for item in probs]
    dvalues = [dot(weight, cotangent).astype(BF16) for weight, cotangent in zip(weights, cotangents)]
    deltas = [
        jnp.sum(weight.astype(F32) * dprob, axis=0, keepdims=True) for weight, dprob in zip(weights, dprobs)
    ]
    dscores = [
        (prob * (dprob - delta)).astype(BF16) for prob, dprob, delta in zip(probs, dprobs, deltas)
    ]
    dkeys = [(dot(dscore, query) * SCALE).astype(BF16) for dscore, query in zip(dscores, queries)]
    dqueries = [(dot_first(dscore, key) * SCALE).astype(BF16) for dscore, key in zip(dscores, keys)]
    return list(zip(dqueries, dkeys, dvalues))


def causal(keys, queries, ahead):
    row = lax.broadcasted_iota(jnp.int32, (keys, queries), 0)
    column = lax.broadcasted_iota(jnp.int32, (keys, queries), 1)
    return row <= column + ahead


def lanes_of(info_ref, slot, block=0):
    return pl.ds(pl.multiple_of(info_ref[2 + slot] * HEAD + block * WIDTH, HEAD), HEAD)


def spread(ref, place):
    parts = [ref if item == place else jnp.zeros_like(ref) for item in range(4)]
    return jnp.concatenate(parts, axis=0)


def prepare(
    info_ref, key_ref, value_ref, normed_ref, down_ref, send_ref, low_ref, pair_own, normed_own, down_own, *sems
):
    pair_copies, wide_copies = [], []
    for item, source in enumerate((key_ref, value_ref)):
        copy = pltpu.make_async_copy(source.at[HALF:], pair_own.at[item], sems[0].at[item])
        copy.start()
        pair_copies.append(copy)
    span = MODEL // WIDE
    for part in range(WIDE):
        lanes = slice(part * span, (part + 1) * span)
        for item, (source, target) in enumerate(((normed_ref, normed_own), (down_ref, down_own))):
            copy = pltpu.make_async_copy(source.at[:, lanes], target.at[:, lanes], sems[1].at[item, part])
            copy.start()
            wide_copies.append(copy)
    for item in range(2):
        pair_copies[item].wait()
        for slot in range(SHIFTED):
            place = item * SHIFTED + slot
            send_ref[:, place * HEAD : (place + 1) * HEAD] = pair_own[item, :, lanes_of(info_ref, slot)]
    low = jnp.zeros((ROWS, 3 * RANK), F32)
    for part in range(WIDE):
        lanes = slice(part * span, (part + 1) * span)
        for copy in wide_copies[2 * part : 2 * part + 2]:
            copy.wait()
        low = low + dot_last(normed_own[:, lanes], down_own[:, lanes])
    low = jnp.concatenate([low.astype(BF16), jnp.zeros((ROWS, HEAD - 3 * RANK), BF16)], axis=1)
    low_ref[...] = low
    send_ref[:, 2 * SHIFTED * HEAD :] = low[HALF:]


def outer_kernel(info_ref, *refs):
    @pl.when(info_ref[0] == 1)
    def _():
        prepare(info_ref, *refs)


def inner_kernel(info_ref, have_ref, *refs):
    @pl.when(info_ref[0] == 0)
    def _():
        prepare(info_ref, *refs)

    @pl.when(info_ref[0] == 1)
    def _():
        refs[5][...] = have_ref[...]


def own_work(info_ref, query_ref, key_ref, value_ref, cot_ref, up_ref, out_ref, proj_ref):
    refs = (query_ref, key_ref, value_ref, cot_ref)
    whole = causal(ROWS, ROWS, 0)
    half = causal(HALF, HALF, 0)
    nothing = jnp.zeros((HALF, HEAD), BF16)
    for start in range(SHIFTED, HEADS, BATCH):
        slots = range(start, start + BATCH)
        grads = attend([[ref[:, lanes_of(info_ref, slot)] for ref in refs] for slot in slots], whole)
        for slot, parts in zip(slots, grads):
            for block in range(3):
                out_ref[:, lanes_of(info_ref, slot, block)] = parts[block]
    for start in range(0, SHIFTED, BATCH):
        slots = range(start, start + BATCH)
        grads = attend([[ref[HALF:, lanes_of(info_ref, slot)] for ref in refs] for slot in slots], half)
        for slot, parts in zip(slots, grads):
            for block in range(3):
                out_ref[:HALF, lanes_of(info_ref, slot, block)] = nothing
                out_ref[HALF:, lanes_of(info_ref, slot, block)] = parts[block]
    total = jnp.zeros((ROWS, HEAD), F32)
    for block in range(3):
        columns = slice(block * WIDTH, (block + 1) * WIDTH)
        total = total + dot_last(out_ref[:, columns], spread(up_ref[:, columns], block))
    proj_ref[...] = total


def joint_work(
    info_ref, query_ref, key_ref, value_ref, cot_ref, come_ref, up_ref, have_ref, late_ref, proj_ref, back_ref, far_ref
):
    far_ref[...] = come_ref[:, 2 * SHIFTED * HEAD :]
    allowed = causal(ROWS, HALF, HALF)
    nothing = jnp.zeros((HALF, HEAD), BF16)
    width = SHIFTED * HEAD
    for start in range(0, SHIFTED, BATCH):
        slots = range(start, start + BATCH)
        parts = []
        for slot in slots:
            lanes = lanes_of(info_ref, slot)
            key, value = (
                jnp.concatenate([come_ref[:, place * HEAD : (place + 1) * HEAD], ref[:HALF, lanes]], axis=0)
                for place, ref in ((slot, key_ref), (SHIFTED + slot, value_ref))
            )
            parts.append([query_ref[:HALF, lanes], key, value, cot_ref[:HALF, lanes]])
        for slot, (dquery, dkey, dvalue) in zip(slots, attend(parts, allowed)):
            lanes = slice(slot * HEAD, (slot + 1) * HEAD)
            late_ref[:HALF, lanes] = dquery
            late_ref[HALF:, lanes] = nothing
            for block, grad in ((1, dkey), (2, dvalue)):
                lanes = slice(block * width + slot * HEAD, block * width + (slot + 1) * HEAD)
                late_ref[:HALF, lanes] = grad[HALF:]
                late_ref[HALF:, lanes] = grad[:HALF]
    total = jnp.zeros((ROWS, HEAD), F32)
    for block in range(3):
        up = jnp.concatenate([up_ref[:, lanes_of(info_ref, slot, block)] for slot in range(SHIFTED)], axis=1)
        total = total + dot_last(late_ref[:, block * width : (block + 1) * width], spread(up, block))
    proj_ref[...] = jnp.concatenate([have_ref[:HALF] + total[:HALF], have_ref[HALF:]], axis=0)
    back_ref[...] = total[HALF:]


def own_kernel(info_ref, *refs):
    @pl.when(info_ref[0] == 0)
    def _():
        own_work(info_ref, *refs)


def joint_kernel(info_ref, *refs):
    @pl.when(info_ref[0] == 0)
    def _():
        joint_work(info_ref, *refs)


def later_kernel(
    info_ref, query_ref, key_ref, value_ref, cot_ref, come_ref, up_ref, ready_ref, grads_ref, *refs
):
    del ready_ref
    refs, have_ref = refs[:-1], refs[-1]
    inputs = (info_ref, query_ref, key_ref, value_ref, cot_ref)

    @pl.when(info_ref[0] == 1)
    def _():
        own_work(*inputs, up_ref, grads_ref, have_ref)
        joint_work(*inputs, come_ref, up_ref, have_ref, *refs)


def accumulate(info_ref, grads_ref, late_ref, far_ref, low_ref, sums_ref):
    span = WIDTH // 4
    low = low_ref[...]
    far_low = jnp.concatenate([low[:HALF], far_ref[...]], axis=0)
    for block in range(3):
        right, far_right = (
            jnp.concatenate([item[:, block * RANK : (block + 1) * RANK]] * 4, axis=1) for item in (low, far_low)
        )
        for chunk in range(4 * block, 4 * block + 4):
            columns = slice(chunk * span, (chunk + 1) * span)
            sums_ref[columns, :] = dot_first(grads_ref[:, columns], right)
        for slot in range(SHIFTED):
            start = (block * SHIFTED + slot) * HEAD
            sums_ref[lanes_of(info_ref, slot, block), :] += dot_first(late_ref[:, start : start + HEAD], far_right)


def up_kernel(info_ref, *refs):
    parts, (low_ref, out_ref, sums_ref) = (refs[:3], refs[3:6]), refs[6:]
    for core in range(C):

        @pl.when(info_ref[0] == core)
        def _():
            accumulate(info_ref, *parts[core], low_ref, sums_ref)

    place = lax.broadcasted_iota(jnp.int32, (8, HEAD), 1) // RANK
    upper = lax.broadcasted_iota(jnp.int32, (8, HEAD), 0) < 4

    def tile(z, g, third):
        start = ((z * G + g) * 3 + third) * 8
        return sums_ref[start : start + 8, :]

    for g in range(G):
        for z in range(0, Z, 2):
            for c in range(C):
                pair = jnp.concatenate([tile(z, g, 2 * c), tile(z + 1, g, 2 * c)], axis=0)
                out_ref[c, g, z * 8 : z * 8 + 16, :] = pair.astype(BF16)
        middle = []
        for low_z in range(BAND):
            merged = tile(low_z, g, 1)
            for quarter in range(1, 4):
                merged = jnp.where(place == quarter, tile(BAND * quarter + low_z, g, 1), merged)
            middle.append(merged)
        swapped = [pltpu.roll(item, 4, 0) for item in middle]
        for c in range(C):
            rows = []
            for even in range(0, BAND, 2):
                if c == 0:
                    rows.append(jnp.where(upper, middle[even], swapped[even + 1]))
                else:
                    rows.append(jnp.where(upper, swapped[even], middle[even + 1]))
            out_ref[c, g, Z * 8 :, :] = jnp.concatenate(rows, axis=0).astype(BF16)


def down_kernel(info_ref, normed_ref, first_ref, later_ref, outer_ref, inner_ref, up_ref, mine_ref, other_ref):
    own = info_ref[0]
    total = jnp.where(own == 0, first_ref[...], later_ref[...])
    back = jnp.where(own == 0, inner_ref[...], outer_ref[...])
    total = jnp.concatenate([total[:HALF], total[HALF:] + back], axis=0).astype(BF16)
    lane = lax.broadcasted_iota(jnp.int32, (16, HEAD), 1)
    for z in range(0, Z, 2):
        part = dot_first(normed_ref[:, z * G * 16 : (z + 2) * G * 16], total)
        part = part.reshape(2, G, C, 8, HEAD)
        for g in range(G):
            pieces = []
            for c in range(C):
                down = jnp.concatenate([part[0, g, c], part[1, g, c]], axis=0)
                up = up_ref[c, g, z * 8 : z * 8 + 16, :]
                pieces.append(jnp.where(lane < 3 * RANK, down, up.astype(F32)).astype(BF16))
            start = g * PART + z * 8
            mine_ref[start : start + 16, :] = jnp.where(own == 0, pieces[0], pieces[1])
            other_ref[start : start + 16, :] = jnp.where(own == 0, pieces[1], pieces[0])
    for g in range(G):
        span = slice(g * PART + Z * 8, (g + 1) * PART)
        pieces = [up_ref[c, g, Z * 8 :, :] for c in range(C)]
        mine_ref[span, :] = jnp.where(own == 0, pieces[0], pieces[1])
        other_ref[span, :] = jnp.where(own == 0, pieces[1], pieces[0])


def middle_kernel(come_ref, out_ref):
    total = come_ref[0].astype(F32)
    for item in range(1, G):
        total = total + come_ref[item].astype(F32)
    for z in range(Z):
        start = Z * 8 + z % BAND // 2 * 8
        tiles = jnp.concatenate([total[z * 8 : z * 8 + 8], total[start : start + 8]], axis=0)
        out_ref[z] = tiles.astype(BF16)


def last_kernel(info_ref, come_ref, down_ref, up_ref):
    c, z = info_ref[0], info_ref[1]
    total = come_ref[0].astype(F32)
    for item in range(1, Z):
        total = total + come_ref[item].astype(F32)
    total = total * ADAPTER_SCALE
    upper, lower = total[:8], total[8:]
    down_ref[...] = upper[:, : 3 * RANK].astype(BF16)
    lower = pltpu.roll(lower, (3 - z // BAND) * RANK, 1)
    moved = lax.rem(z, 2) != c
    lower = jnp.where(moved, pltpu.roll(lower, 4, 0), lower)
    both = jnp.concatenate([upper, lower], axis=0)
    both = jnp.where(c == 1, pltpu.roll(both, 4, 0), both)
    up_ref[...] = both[:12, 3 * RANK :].astype(BF16)


def shape(dims, kind=BF16):
    return jax.ShapeDtypeStruct(dims, kind)


def prepare_call(body, name, info, extra, keys, values, normed, down):
    return call(
        body,
        name,
        (shape((HALF, (2 * SHIFTED + 1) * HEAD)), shape((ROWS, HEAD))),
        [SMEM] + [VMEM] * len(extra) + [HBM] * 4,
        130_000_000,
        3_000_000,
        limit=53,
        scratch_shapes=[
            pltpu.VMEM((2, HALF, WIDTH), BF16),
            pltpu.VMEM(normed.shape, BF16),
            pltpu.VMEM(down.shape, BF16),
            pltpu.SemaphoreType.DMA((2,)),
            pltpu.SemaphoreType.DMA((2, WIDE)),
        ],
    )(info, *extra, keys, values, normed, down)


OWN = (shape((ROWS, 3 * WIDTH)), shape((ROWS, HEAD), F32))
JOINT = (shape((ROWS, 3 * SHIFTED * HEAD)), shape((ROWS, HEAD), F32), shape((HALF, HEAD), F32), shape((HALF, HEAD)))


def own_call(info, *inputs):
    return call(own_kernel, "own_attention", OWN, [SMEM] + [VMEM] * 5, 2_000_000_000, 6_000_000)(info, *inputs)


def joint_call(info, *inputs):
    return call(joint_kernel, "joint_attention", JOINT, [SMEM] + [VMEM] * 7, 1_000_000_000, 4_000_000)(info, *inputs)


def later_call(info, *inputs):
    return call(
        later_kernel,
        "later_attention",
        (OWN[0], *JOINT),
        [SMEM] + [VMEM] * 7,
        3_000_000_000,
        8_000_000,
        scratch_shapes=[pltpu.VMEM((ROWS, HEAD), F32)],
    )(info, *inputs)


def up_call(info, *inputs):
    return call(
        up_kernel,
        "up_gradient",
        shape((C, G, PART, HEAD)),
        [SMEM] + [VMEM] * 7,
        1_000_000_000,
        6_000_000,
        scratch_shapes=[pltpu.VMEM((3 * WIDTH, HEAD), F32)],
    )(info, *inputs)


def down_call(info, *inputs):
    return call(
        down_kernel,
        "down_gradient",
        (shape((G * PART, HEAD)), shape((G * PART, HEAD))),
        [SMEM] + [VMEM] * 6,
        500_000_000,
        4_000_000,
    )(info, *inputs)


def middle_call(come):
    return call(middle_kernel, "middle_sum", shape((Z, 16, HEAD)), [VMEM], 1_000_000, 600_000)(come)


def last_call(info, come):
    return call(
        last_kernel, "last_sum", (shape((8, 3 * RANK)), shape((12, RANK))), [SMEM, VMEM], 100_000, 70_000
    )(info, come)


def per_device(normed, queries, keys, values, cotangent, down, up, order):
    normed, queries, keys, values, cotangent = (
        item[0] for item in (normed, queries, keys, values, cotangent)
    )
    ring = ("yh", "x", "c")
    count = 16
    ahead = [(item, (item + 1) % count) for item in range(count)]
    behind = [(item, (item - 1) % count) for item in range(count)]
    info = jnp.concatenate([jnp.stack([lax.axis_index("c"), lax.axis_index(FAR)]), order])
    sources = (keys, values, normed, down.T)
    inputs = (queries, keys, values, cotangent)
    send, low = prepare_call(outer_kernel, "outer_parts", info, (), *sources)
    outer = lax.ppermute(send, ring, ahead[1::2])
    send, low = prepare_call(inner_kernel, "inner_parts", info, (low,), *sources)
    inner = lax.ppermute(send, ring, ahead[::2])
    grads, have = own_call(info, *inputs, up)
    late, proj, back, far = joint_call(info, *inputs, outer, up, have)
    outer_back = lax.ppermute(back, ring, behind[::2])
    later = later_call(info, *inputs, inner, up, far)
    inner_back = lax.ppermute(later[3], ring, behind[1::2])
    up_part = up_call(info, grads, late, far, later[0], later[1], later[4], low)
    mine, other = down_call(info, normed, proj, later[2], outer_back, inner_back, up_part)
    other = lax.ppermute(other, "c", [(0, 1), (1, 0)])
    chip = (mine.astype(F32) + other.astype(F32)).astype(BF16)
    plane = lax.all_to_all(chip.reshape(G, PART, HEAD), NEAR, 0, 0)
    line = lax.all_to_all(middle_call(plane), FAR, 0, 0)
    down_grad, up_grad = last_call(info, line)
    return down_grad, up_grad.T


def solution(mesh):
    fine = Mesh(mesh.devices.reshape(16, 2, 2, 4, 2), ("z", "yl", "yh", "x", "c"))
    dp, seq = ("z", "yl"), ("yh", "x", "c")
    tokens = P(dp, seq, None)
    in_specs = (tokens,) * 5 + (P(),) * 3
    out_specs = (P(dp + seq, None), P(None, dp + seq))
    return jax.shard_map(per_device, mesh=fine, in_specs=in_specs, out_specs=out_specs, check_vma=False)
```

```python
import jax
import jax.numpy as jnp
from jax import lax
from jax.experimental import pallas as pl
from jax.experimental.pallas import tpu as pltpu
from jax.sharding import Mesh
from jax.sharding import PartitionSpec as P

HEAD = 128
ROWS = 160
HALF = 80
HEADS = 16
SHIFTED = 8
WIDTH = HEADS * HEAD
MODEL = 4096
RANK = 32
SCALE = HEAD ** -0.5
ADAPTER_SCALE = 0.25
NEAR, FAR = ("yl", "yh", "x"), ("z",)
Z, G, C = 16, 16, 2
BAND = Z // 4
WIDE = 2
NARROW = SHIFTED * HEAD
PART = Z * 8 + BAND * 4

BF16, F32 = jnp.bfloat16, jnp.float32
VMEM = pl.BlockSpec(memory_space=pltpu.VMEM)
HBM = pl.BlockSpec(memory_space=pltpu.HBM)
ANY = pl.BlockSpec(memory_space=pl.ANY)
ORDER = (pltpu.SMEM((HEADS,), jnp.int32), pltpu.SemaphoreType.DMA)


def call(body, name, out_shape, in_specs, flops, size, limit=32, out_specs=None, **rest):
    return pl.pallas_call(
        body,
        name=name,
        out_shape=out_shape,
        in_specs=in_specs,
        out_specs=out_specs or jax.tree.map(lambda _: VMEM, out_shape),
        compiler_params=pltpu.CompilerParams(vmem_limit_bytes=limit * 1024 * 1024),
        cost_estimate=pl.CostEstimate(flops=flops, bytes_accessed=size, transcendentals=0),
        **rest,
    )


def dot(left, right):
    return jnp.dot(left, right, preferred_element_type=F32)


def dot_last(left, right):
    return lax.dot_general(left, right, (((1,), (1,)), ((), ())), preferred_element_type=F32)


def dot_first(left, right):
    return lax.dot_general(left, right, (((0,), (0,)), ((), ())), preferred_element_type=F32)


def attend(parts, allowed):
    queries, keys, values, cotangents = zip(*parts)
    scores = [jnp.where(allowed, dot_last(key, query), -jnp.inf) for query, key in zip(queries, keys)]
    dprobs = [dot_last(value, cotangent) for value, cotangent in zip(values, cotangents)]
    tops = [jnp.max(item, axis=0, keepdims=True) for item in scores]
    powers = [jnp.exp((item - top) * SCALE) for item, top in zip(scores, tops)]
    probs = [item * (1.0 / jnp.sum(item, axis=0, keepdims=True)) for item in powers]
    weights = [item.astype(BF16) for item in probs]
    dvalues = [dot(weight, cotangent).astype(BF16) for weight, cotangent in zip(weights, cotangents)]
    deltas = [
        jnp.sum(weight.astype(F32) * dprob, axis=0, keepdims=True) for weight, dprob in zip(weights, dprobs)
    ]
    dscores = [
        (prob * (dprob - delta)).astype(BF16) for prob, dprob, delta in zip(probs, dprobs, deltas)
    ]
    dkeys = [(dot(dscore, query) * SCALE).astype(BF16) for dscore, query in zip(dscores, queries)]
    dqueries = [(dot_first(dscore, key) * SCALE).astype(BF16) for dscore, key in zip(dscores, keys)]
    return list(zip(dqueries, dkeys, dvalues))


def causal(keys, queries, ahead):
    row = lax.broadcasted_iota(jnp.int32, (keys, queries), 0)
    column = lax.broadcasted_iota(jnp.int32, (keys, queries), 1)
    return row <= column + ahead


def lanes_of(order_ref, slot, block=0):
    return pl.ds(pl.multiple_of(order_ref[slot] * HEAD + block * WIDTH, HEAD), HEAD)


def narrow_lanes(slot, block=0):
    return slice(block * NARROW + slot * HEAD, block * NARROW + (slot + 1) * HEAD)


def fetch(source_ref, order_ref, sem):
    copy = pltpu.make_async_copy(source_ref, order_ref, sem)
    copy.start()
    return copy


def prepare(
    source_ref,
    key_ref,
    value_ref,
    normed_ref,
    down_ref,
    send_ref,
    low_ref,
    pair_own,
    normed_own,
    down_own,
    pair_sems,
    wide_sems,
    order_ref,
    order_sem,
):
    order_copy = fetch(source_ref, order_ref, order_sem)
    pair_copies, wide_copies = [], []
    for item, source in enumerate((key_ref, value_ref)):
        copy = pltpu.make_async_copy(source.at[HALF:], pair_own.at[item], pair_sems.at[item])
        copy.start()
        pair_copies.append(copy)
    span = MODEL // WIDE
    for part in range(WIDE):
        lanes = slice(part * span, (part + 1) * span)
        for item, (source, target) in enumerate(((normed_ref, normed_own), (down_ref, down_own))):
            copy = pltpu.make_async_copy(source.at[:, lanes], target.at[:, lanes], wide_sems.at[item, part])
            copy.start()
            wide_copies.append(copy)
    order_copy.wait()
    for item in range(2):
        pair_copies[item].wait()
        for slot in range(SHIFTED):
            place = item * SHIFTED + slot
            send_ref[:, place * HEAD : (place + 1) * HEAD] = pair_own[item, :, lanes_of(order_ref, slot)]
    low = jnp.zeros((ROWS, 3 * RANK), F32)
    for part in range(WIDE):
        lanes = slice(part * span, (part + 1) * span)
        for copy in wide_copies[2 * part : 2 * part + 2]:
            copy.wait()
        low = low + dot_last(normed_own[:, lanes], down_own[:, lanes])
    low = jnp.concatenate([low.astype(BF16), jnp.zeros((ROWS, HEAD - 3 * RANK), BF16)], axis=1)
    low_ref[...] = low
    send_ref[:, 2 * SHIFTED * HEAD :] = low[HALF:]


def outer_kernel(*refs):
    @pl.when(lax.axis_index("c") == 1)
    def _():
        prepare(*refs)


def inner_kernel(have_ref, *refs):
    core = lax.axis_index("c")

    @pl.when(core == 0)
    def _():
        prepare(*refs)

    @pl.when(core == 1)
    def _():
        refs[6][...] = have_ref[...]


def project(order_ref, grads_ref, up_ref, slots):
    total = jnp.zeros((grads_ref.shape[0], HEAD), F32)
    for block in range(3):
        up = jnp.concatenate([up_ref[:, lanes_of(order_ref, slot, block)] for slot in slots], axis=1)
        parts = [up if place == block else jnp.zeros_like(up) for place in range(4)]
        columns = slice(block * NARROW, (block + 1) * NARROW)
        total = total + dot_last(grads_ref[:, columns], jnp.concatenate(parts, axis=0))
    return total


def half_work(order_ref, refs, up_ref, half_ref, half_proj_ref):
    slots = range(SHIFTED)
    parts = [[ref[HALF:, lanes_of(order_ref, slot)] for ref in refs] for slot in slots]
    for slot, grads in zip(slots, attend(parts, causal(HALF, HALF, 0))):
        for block in range(3):
            half_ref[:, narrow_lanes(slot, block)] = grads[block]
    half_proj_ref[...] = project(order_ref, half_ref, up_ref, slots)


def plain_work(order_ref, refs, up_ref, plain_ref, plain_proj_ref):
    slots = range(SHIFTED, HEADS)
    parts = [[ref[:, lanes_of(order_ref, slot)] for ref in refs] for slot in slots]
    for slot, grads in zip(slots, attend(parts, causal(ROWS, ROWS, 0))):
        for block in range(3):
            plain_ref[:, narrow_lanes(slot - SHIFTED, block)] = grads[block]
    plain_proj_ref[...] = project(order_ref, plain_ref, up_ref, slots)


def joint_work(
    order_ref, refs, come_ref, up_ref, plain_proj_ref, half_proj_ref, late_ref, proj_ref, back_ref, far_ref
):
    query_ref, key_ref, value_ref, cot_ref = refs
    far_ref[...] = come_ref[:, 2 * SHIFTED * HEAD :]
    nothing = jnp.zeros((HALF, HEAD), BF16)
    slots = range(SHIFTED)
    parts = []
    for slot in slots:
        lanes = lanes_of(order_ref, slot)
        key, value = (
            jnp.concatenate([come_ref[:, place * HEAD : (place + 1) * HEAD], ref[:HALF, lanes]], axis=0)
            for place, ref in ((slot, key_ref), (SHIFTED + slot, value_ref))
        )
        parts.append([query_ref[:HALF, lanes], key, value, cot_ref[:HALF, lanes]])
    for slot, (dquery, dkey, dvalue) in zip(slots, attend(parts, causal(ROWS, HALF, HALF))):
        late_ref[:HALF, narrow_lanes(slot)] = dquery
        late_ref[HALF:, narrow_lanes(slot)] = nothing
        for block, grad in ((1, dkey), (2, dvalue)):
            late_ref[:HALF, narrow_lanes(slot, block)] = grad[HALF:]
            late_ref[HALF:, narrow_lanes(slot, block)] = grad[:HALF]
    total = project(order_ref, late_ref, up_ref, slots)
    plain = plain_proj_ref[...]
    proj_ref[...] = jnp.concatenate([plain[:HALF] + total[:HALF], plain[HALF:] + half_proj_ref[...]], axis=0)
    back_ref[...] = total[HALF:]


def own_kernel(*refs):
    source_ref, inputs, up_ref = refs[0], refs[1:5], refs[5]
    half_refs, plain_refs, (order_ref, order_sem) = refs[6:8], refs[8:10], refs[10:]
    fetch(source_ref, order_ref, order_sem).wait()

    @pl.when(lax.axis_index("c") == 0)
    def _():
        plain_work(order_ref, inputs, up_ref, *plain_refs)

    half_work(order_ref, inputs, up_ref, *half_refs)


def joint_kernel(*refs):
    source_ref, inputs, rest, (order_ref, order_sem) = refs[0], refs[1:5], refs[5:-2], refs[-2:]

    @pl.when(lax.axis_index("c") == 0)
    def _():
        fetch(source_ref, order_ref, order_sem).wait()
        joint_work(order_ref, inputs, *rest)


def later_kernel(*refs):
    source_ref, inputs, come_ref, up_ref, half_proj_ref = refs[0], refs[1:5], refs[5], refs[6], refs[7]
    plain_ref, outs, (plain_proj_ref, order_ref, order_sem) = refs[9], refs[10:14], refs[14:]

    @pl.when(lax.axis_index("c") == 1)
    def _():
        fetch(source_ref, order_ref, order_sem).wait()
        plain_work(order_ref, inputs, up_ref, plain_ref, plain_proj_ref)
        joint_work(order_ref, inputs, come_ref, up_ref, plain_proj_ref, half_proj_ref, *outs)


def accumulate(order_ref, order_copy, plain_ref, late_ref, far_ref, half_ref, low_ref, sums_ref):
    low = low_ref[...]
    late_low = jnp.concatenate([low[:HALF], far_ref[...], low[HALF:]], axis=0)
    rights = [
        [jnp.concatenate([item[:, block * RANK : (block + 1) * RANK]] * 4, axis=1) for block in range(3)]
        for item in (low, late_low)
    ]
    order_copy.wait()
    for block in range(3):
        for slot in range(SHIFTED):
            lanes = narrow_lanes(slot, block)
            sums_ref[lanes_of(order_ref, SHIFTED + slot, block), :] = dot_first(plain_ref[:, lanes], rights[0][block])
            left = jnp.concatenate([late_ref[:, lanes], half_ref[:, lanes]], axis=0)
            sums_ref[lanes_of(order_ref, slot, block), :] = dot_first(left, rights[1][block])


def up_kernel(*refs):
    source_ref, parts, half_ref, low_ref = refs[0], (refs[1:4], refs[4:7]), refs[7], refs[8]
    out_ref, sums_ref, order_ref, order_sem = refs[9:]
    order_copy = fetch(source_ref, order_ref, order_sem)
    for core in range(C):

        @pl.when(lax.axis_index("c") == core)
        def _():
            accumulate(order_ref, order_copy, *parts[core], half_ref, low_ref, sums_ref)

    place = lax.broadcasted_iota(jnp.int32, (8, HEAD), 1) // RANK
    upper = lax.broadcasted_iota(jnp.int32, (8, HEAD), 0) < 4

    def tile(z, g, third):
        start = ((z * G + g) * 3 + third) * 8
        return sums_ref[start : start + 8, :]

    for g in range(G):
        for z in range(0, Z, 2):
            for c in range(C):
                pair = jnp.concatenate([tile(z, g, 2 * c), tile(z + 1, g, 2 * c)], axis=0)
                out_ref[c, g, z * 8 : z * 8 + 16, :] = pair.astype(BF16)
        middle = []
        for low_z in range(BAND):
            merged = tile(low_z, g, 1)
            for quarter in range(1, 4):
                merged = jnp.where(place == quarter, tile(BAND * quarter + low_z, g, 1), merged)
            middle.append(merged)
        swapped = [pltpu.roll(item, 4, 0) for item in middle]
        for c in range(C):
            rows = []
            for even in range(0, BAND, 2):
                if c == 0:
                    rows.append(jnp.where(upper, middle[even], swapped[even + 1]))
                else:
                    rows.append(jnp.where(upper, swapped[even], middle[even + 1]))
            out_ref[c, g, Z * 8 :, :] = jnp.concatenate(rows, axis=0).astype(BF16)


def down_kernel(normed_ref, first_ref, later_ref, outer_ref, inner_ref, up_ref, mine_ref, other_ref):
    own = lax.axis_index("c")
    total = jnp.where(own == 0, first_ref[...], later_ref[...])
    back = jnp.where(own == 0, inner_ref[...], outer_ref[...])
    total = jnp.concatenate([total[:HALF], total[HALF:] + back], axis=0).astype(BF16)
    lane = lax.broadcasted_iota(jnp.int32, (16, HEAD), 1)
    for z in range(0, Z, 2):
        part = dot_first(normed_ref[:, z * G * 16 : (z + 2) * G * 16], total)
        part = part.reshape(2, G, C, 8, HEAD)
        for g in range(G):
            pieces = []
            for c in range(C):
                down = jnp.concatenate([part[0, g, c], part[1, g, c]], axis=0)
                up = up_ref[c, g, z * 8 : z * 8 + 16, :]
                pieces.append(jnp.where(lane < 3 * RANK, down, up.astype(F32)).astype(BF16))
            start = g * PART + z * 8
            mine_ref[start : start + 16, :] = jnp.where(own == 0, pieces[0], pieces[1])
            other_ref[start : start + 16, :] = jnp.where(own == 0, pieces[1], pieces[0])
    for g in range(G):
        span = slice(g * PART + Z * 8, (g + 1) * PART)
        pieces = [up_ref[c, g, Z * 8 :, :] for c in range(C)]
        mine_ref[span, :] = jnp.where(own == 0, pieces[0], pieces[1])
        other_ref[span, :] = jnp.where(own == 0, pieces[1], pieces[0])


def middle_kernel(come_ref, out_ref):
    total = come_ref[0].astype(F32)
    for item in range(1, G):
        total = total + come_ref[item].astype(F32)
    for z in range(Z):
        start = Z * 8 + z % BAND // 2 * 8
        tiles = jnp.concatenate([total[z * 8 : z * 8 + 8], total[start : start + 8]], axis=0)
        out_ref[z] = tiles.astype(BF16)


def last_kernel(come_ref, down_ref, up_ref):
    c, z = lax.axis_index("c"), lax.axis_index(FAR)
    total = come_ref[0].astype(F32)
    for item in range(1, Z):
        total = total + come_ref[item].astype(F32)
    total = total * ADAPTER_SCALE
    upper, lower = total[:8], total[8:]
    down_ref[...] = upper[:, : 3 * RANK].astype(BF16)
    lower = pltpu.roll(lower, (3 - z // BAND) * RANK, 1)
    moved = lax.rem(z, 2) != c
    lower = jnp.where(moved, pltpu.roll(lower, 4, 0), lower)
    both = jnp.concatenate([upper, lower], axis=0)
    both = jnp.where(c == 1, pltpu.roll(both, 4, 0), both)
    up_ref[...] = both[:12, 3 * RANK :].astype(BF16)


def shape(dims, kind=BF16):
    return jax.ShapeDtypeStruct(dims, kind)


def prepare_call(body, name, extra, order, keys, values, normed, down):
    return call(
        body,
        name,
        (shape((HALF, (2 * SHIFTED + 1) * HEAD)), shape((ROWS, HEAD))),
        [VMEM] * len(extra) + [ANY] + [HBM] * 4,
        130_000_000,
        3_000_000,
        limit=53,
        scratch_shapes=[
            pltpu.VMEM((2, HALF, WIDTH), BF16),
            pltpu.VMEM(normed.shape, BF16),
            pltpu.VMEM(down.shape, BF16),
            pltpu.SemaphoreType.DMA((2,)),
            pltpu.SemaphoreType.DMA((2, WIDE)),
            *ORDER,
        ],
    )(*extra, order, keys, values, normed, down)


PLAIN = (shape((ROWS, 3 * NARROW)), shape((ROWS, HEAD), F32))
HALVES = (shape((HALF, 3 * NARROW)), shape((HALF, HEAD), F32))
JOINT = (shape((ROWS, 3 * NARROW)), shape((ROWS, HEAD), F32), shape((HALF, HEAD), F32), shape((HALF, HEAD)))


def work_call(body, name, out_shape, inputs, flops, scratch=()):
    return call(
        body,
        name,
        out_shape,
        [ANY] + [VMEM] * (len(inputs) - 1),
        flops,
        6_000_000,
        scratch_shapes=[*scratch, *ORDER],
    )(*inputs)


def down_call(*inputs):
    return call(
        down_kernel,
        "down_gradient",
        (shape((G * PART, HEAD)), shape((G * PART, HEAD))),
        [VMEM] * 6,
        500_000_000,
        4_000_000,
    )(*inputs)


def middle_call(come):
    return call(middle_kernel, "middle_sum", shape((Z, 16, HEAD)), [VMEM], 1_000_000, 600_000)(come)


def last_call(come):
    return call(last_kernel, "last_sum", (shape((8, 3 * RANK)), shape((12, RANK))), [VMEM], 100_000, 70_000)(come)


def per_device(normed, queries, keys, values, cotangent, down, up, order):
    normed, queries, keys, values, cotangent = (
        item[0] for item in (normed, queries, keys, values, cotangent)
    )
    ring = ("yh", "x", "c")
    count = 16
    ahead = [(item, (item + 1) % count) for item in range(count)]
    behind = [(item, (item - 1) % count) for item in range(count)]
    sources = (order, keys, values, normed, down.T)
    inputs = (order, queries, keys, values, cotangent)
    send, low = prepare_call(outer_kernel, "outer_parts", (), *sources)
    outer = lax.ppermute(send, ring, ahead[1::2])
    send, low = prepare_call(inner_kernel, "inner_parts", (low,), *sources)
    inner = lax.ppermute(send, ring, ahead[::2])
    half, half_proj, plain, plain_proj = work_call(
        own_kernel, "own_attention", HALVES + PLAIN, (*inputs, up), 2_000_000_000
    )
    late, proj, back, far = work_call(
        joint_kernel, "joint_attention", JOINT, (*inputs, outer, up, plain_proj, half_proj), 1_000_000_000
    )
    outer_back = lax.ppermute(back, ring, behind[::2])
    later = work_call(
        later_kernel,
        "later_attention",
        PLAIN[:1] + JOINT,
        (*inputs, inner, up, half_proj, far),
        3_000_000_000,
        [pltpu.VMEM(PLAIN[1].shape, F32)],
    )
    inner_back = lax.ppermute(later[3], ring, behind[1::2])
    up_part = work_call(
        up_kernel,
        "up_gradient",
        shape((C, G, PART, HEAD)),
        (order, plain, late, far, later[0], later[1], later[4], half, low),
        1_000_000_000,
        [pltpu.VMEM((3 * WIDTH, HEAD), F32)],
    )
    mine, other = down_call(normed, proj, later[2], outer_back, inner_back, up_part)
    other = lax.ppermute(other, "c", [(0, 1), (1, 0)])
    chip = (mine.astype(F32) + other.astype(F32)).astype(BF16)
    plane = lax.all_to_all(chip.reshape(G, PART, HEAD), NEAR, 0, 0)
    line = lax.all_to_all(middle_call(plane), FAR, 0, 0)
    down_grad, up_grad = last_call(line)
    return down_grad, up_grad.T


def solution(mesh):
    fine = Mesh(mesh.devices.reshape(16, 2, 2, 4, 2), ("z", "yl", "yh", "x", "c"))
    dp, seq = ("z", "yl"), ("yh", "x", "c")
    tokens = P(dp, seq, None)
    in_specs = (tokens,) * 5 + (P(),) * 3
    out_specs = (P(dp + seq, None), P(None, dp + seq))
    return jax.shard_map(per_device, mesh=fine, in_specs=in_specs, out_specs=out_specs, check_vma=False)
```

```python
import jax
import jax.numpy as jnp
from jax import lax
from jax.experimental import pallas as pl
from jax.experimental.pallas import tpu as pltpu
from jax.sharding import Mesh
from jax.sharding import PartitionSpec as P

HEAD = 128
ROWS = 160
HALF = 80
HEADS = 16
SHIFTED = 8
WIDTH = HEADS * HEAD
MODEL = 4096
RANK = 32
SCALE = HEAD ** -0.5
ADAPTER_SCALE = 0.25
NEAR, FAR = ("yl", "yh", "x"), ("z",)
Z, G, C = 16, 16, 2
BAND = Z // 4
WIDE = 2
NARROW = SHIFTED * HEAD
PART = Z * 8 + BAND * 4

BF16, F32 = jnp.bfloat16, jnp.float32
VMEM = pl.BlockSpec(memory_space=pltpu.VMEM)
HBM = pl.BlockSpec(memory_space=pltpu.HBM)
ANY = pl.BlockSpec(memory_space=pl.ANY)
ORDER = (pltpu.SMEM((HEADS,), jnp.int32), pltpu.SemaphoreType.DMA)


def call(body, name, out_shape, in_specs, flops, size, limit=32, out_specs=None, **rest):
    return pl.pallas_call(
        body,
        name=name,
        out_shape=out_shape,
        in_specs=in_specs,
        out_specs=out_specs or jax.tree.map(lambda _: VMEM, out_shape),
        compiler_params=pltpu.CompilerParams(vmem_limit_bytes=limit * 1024 * 1024),
        cost_estimate=pl.CostEstimate(flops=flops, bytes_accessed=size, transcendentals=0),
        **rest,
    )


def dot(left, right):
    return jnp.dot(left, right, preferred_element_type=F32)


def dot_last(left, right):
    return lax.dot_general(left, right, (((1,), (1,)), ((), ())), preferred_element_type=F32)


def dot_first(left, right):
    return lax.dot_general(left, right, (((0,), (0,)), ((), ())), preferred_element_type=F32)


def attend(parts, allowed):
    queries, keys, values, cotangents = zip(*parts)
    scores = [jnp.where(allowed, dot_last(key, query), -jnp.inf) for query, key in zip(queries, keys)]
    dprobs = [dot_last(value, cotangent) for value, cotangent in zip(values, cotangents)]
    tops = [jnp.max(item, axis=0, keepdims=True) for item in scores]
    powers = [jnp.exp((item - top) * SCALE) for item, top in zip(scores, tops)]
    probs = [item * (1.0 / jnp.sum(item, axis=0, keepdims=True)) for item in powers]
    weights = [item.astype(BF16) for item in probs]
    dvalues = [dot(weight, cotangent).astype(BF16) for weight, cotangent in zip(weights, cotangents)]
    deltas = [
        jnp.sum(weight.astype(F32) * dprob, axis=0, keepdims=True) for weight, dprob in zip(weights, dprobs)
    ]
    dscores = [
        (prob * (dprob - delta)).astype(BF16) for prob, dprob, delta in zip(probs, dprobs, deltas)
    ]
    dkeys = [(dot(dscore, query) * SCALE).astype(BF16) for dscore, query in zip(dscores, queries)]
    dqueries = [(dot_first(dscore, key) * SCALE).astype(BF16) for dscore, key in zip(dscores, keys)]
    return list(zip(dqueries, dkeys, dvalues))


def causal(keys, queries, ahead):
    row = lax.broadcasted_iota(jnp.int32, (keys, queries), 0)
    column = lax.broadcasted_iota(jnp.int32, (keys, queries), 1)
    return row <= column + ahead


def lanes_of(order_ref, slot, block=0):
    return pl.ds(pl.multiple_of(order_ref[slot] * HEAD + block * WIDTH, HEAD), HEAD)


def narrow_lanes(slot, block=0):
    return slice(block * NARROW + slot * HEAD, block * NARROW + (slot + 1) * HEAD)


def fetch(source_ref, order_ref, sem):
    copy = pltpu.make_async_copy(source_ref, order_ref, sem)
    copy.start()
    return copy


def load_pair(source_ref, key_ref, value_ref, pair_own, pair_sems, order_ref, order_sem):
    copies = [fetch(source_ref, order_ref, order_sem)]
    for item, source in enumerate((key_ref, value_ref)):
        copies.append(fetch(source.at[HALF:], pair_own.at[item], pair_sems.at[item]))
    return copies


def pick_pair(copies, order_ref, pair_own, send_ref):
    copies[0].wait()
    for item in range(2):
        copies[1 + item].wait()
        for slot in range(SHIFTED):
            place = item * SHIFTED + slot
            send_ref[:, place * HEAD : (place + 1) * HEAD] = pair_own[item, :, lanes_of(order_ref, slot)]


def outer_kernel(source_ref, key_ref, value_ref, send_ref, pair_own, pair_sems, order_ref, order_sem):
    @pl.when(lax.axis_index("c") == 1)
    def _():
        copies = load_pair(source_ref, key_ref, value_ref, pair_own, pair_sems, order_ref, order_sem)
        pick_pair(copies, order_ref, pair_own, send_ref)


def inner_kernel(
    source_ref,
    key_ref,
    value_ref,
    normed_ref,
    down_ref,
    send_ref,
    low_ref,
    far_ref,
    normed_own,
    down_own,
    wide_sems,
    pair_own,
    *rest,
):
    pair_sems, order_ref, order_sem = rest
    core = lax.axis_index("c")
    pair = (source_ref, key_ref, value_ref, pair_own, pair_sems, order_ref, order_sem)

    @pl.when(core == 0)
    def _():
        load_pair(*pair)

    wide_copies = []
    span = MODEL // WIDE
    for part in range(WIDE):
        lanes = slice(part * span, (part + 1) * span)
        for item, (source, target) in enumerate(((normed_ref, normed_own), (down_ref, down_own))):
            wide_copies.append(fetch(source.at[:, lanes], target.at[:, lanes], wide_sems.at[item, part]))

    @pl.when(core == 0)
    def _():
        copies = [pltpu.make_async_copy(source_ref, order_ref, order_sem)]
        for item, source in enumerate((key_ref, value_ref)):
            copies.append(pltpu.make_async_copy(source.at[HALF:], pair_own.at[item], pair_sems.at[item]))
        pick_pair(copies, order_ref, pair_own, send_ref)

    low = jnp.zeros((ROWS, 3 * RANK), F32)
    for part in range(WIDE):
        lanes = slice(part * span, (part + 1) * span)
        for copy in wide_copies[2 * part : 2 * part + 2]:
            copy.wait()
        low = low + dot_last(normed_own[:, lanes], down_own[:, lanes])
    low = jnp.concatenate([low.astype(BF16), jnp.zeros((ROWS, HEAD - 3 * RANK), BF16)], axis=1)
    low_ref[...] = low
    far_ref[...] = low[HALF:]
    send_ref[:, 2 * SHIFTED * HEAD :] = low[HALF:]


def project(order_ref, grads_ref, up_ref, slots):
    total = jnp.zeros((grads_ref.shape[0], HEAD), F32)
    for block in range(3):
        up = jnp.concatenate([up_ref[:, lanes_of(order_ref, slot, block)] for slot in slots], axis=1)
        parts = [up if place == block else jnp.zeros_like(up) for place in range(4)]
        columns = slice(block * NARROW, (block + 1) * NARROW)
        total = total + dot_last(grads_ref[:, columns], jnp.concatenate(parts, axis=0))
    return total


def half_work(order_ref, refs, up_ref, half_ref, half_proj_ref):
    slots = range(SHIFTED)
    parts = [[ref[HALF:, lanes_of(order_ref, slot)] for ref in refs] for slot in slots]
    for slot, grads in zip(slots, attend(parts, causal(HALF, HALF, 0))):
        for block in range(3):
            half_ref[:, narrow_lanes(slot, block)] = grads[block]
    half_proj_ref[...] = project(order_ref, half_ref, up_ref, slots)


def plain_work(order_ref, refs, up_ref, plain_ref, plain_proj_ref):
    slots = range(SHIFTED, HEADS)
    parts = [[ref[:, lanes_of(order_ref, slot)] for ref in refs] for slot in slots]
    for slot, grads in zip(slots, attend(parts, causal(ROWS, ROWS, 0))):
        for block in range(3):
            plain_ref[:, narrow_lanes(slot - SHIFTED, block)] = grads[block]
    plain_proj_ref[...] = project(order_ref, plain_ref, up_ref, slots)


def joint_work(
    order_ref, refs, come_ref, up_ref, plain_proj_ref, half_proj_ref, late_ref, proj_ref, back_ref
):
    query_ref, key_ref, value_ref, cot_ref = refs
    nothing = jnp.zeros((HALF, HEAD), BF16)
    slots = range(SHIFTED)
    parts = []
    for slot in slots:
        lanes = lanes_of(order_ref, slot)
        key, value = (
            jnp.concatenate([come_ref[:, place * HEAD : (place + 1) * HEAD], ref[:HALF, lanes]], axis=0)
            for place, ref in ((slot, key_ref), (SHIFTED + slot, value_ref))
        )
        parts.append([query_ref[:HALF, lanes], key, value, cot_ref[:HALF, lanes]])
    for slot, (dquery, dkey, dvalue) in zip(slots, attend(parts, causal(ROWS, HALF, HALF))):
        late_ref[:HALF, narrow_lanes(slot)] = dquery
        late_ref[HALF:, narrow_lanes(slot)] = nothing
        for block, grad in ((1, dkey), (2, dvalue)):
            late_ref[:HALF, narrow_lanes(slot, block)] = grad[HALF:]
            late_ref[HALF:, narrow_lanes(slot, block)] = grad[:HALF]
    total = project(order_ref, late_ref, up_ref, slots)
    plain = plain_proj_ref[...]
    proj_ref[...] = jnp.concatenate([plain[:HALF] + total[:HALF], plain[HALF:] + half_proj_ref[...]], axis=0)
    back_ref[...] = total[HALF:]


def own_kernel(*refs):
    source_ref, inputs, up_ref = refs[0], refs[1:5], refs[5]
    half_refs, plain_refs, (order_ref, order_sem) = refs[6:8], refs[8:10], refs[10:]
    fetch(source_ref, order_ref, order_sem).wait()

    @pl.when(lax.axis_index("c") == 0)
    def _():
        plain_work(order_ref, inputs, up_ref, *plain_refs)

    half_work(order_ref, inputs, up_ref, *half_refs)


def joint_kernel(*refs):
    source_ref, inputs, rest, (order_ref, order_sem) = refs[0], refs[1:5], refs[5:-2], refs[-2:]

    @pl.when(lax.axis_index("c") == 0)
    def _():
        fetch(source_ref, order_ref, order_sem).wait()
        joint_work(order_ref, inputs, *rest)


def later_kernel(*refs):
    source_ref, inputs, come_ref, up_ref, half_proj_ref = refs[0], refs[1:5], refs[5], refs[6], refs[7]
    plain_ref, outs, (plain_proj_ref, order_ref, order_sem) = refs[9], refs[10:13], refs[13:]

    @pl.when(lax.axis_index("c") == 1)
    def _():
        fetch(source_ref, order_ref, order_sem).wait()
        plain_work(order_ref, inputs, up_ref, plain_ref, plain_proj_ref)
        joint_work(order_ref, inputs, come_ref, up_ref, plain_proj_ref, half_proj_ref, *outs)


def accumulate(order_ref, order_copy, plain_ref, late_ref, far_ref, half_ref, low_ref, sums_ref):
    low = low_ref[...]
    far_low = far_ref[:, far_ref.shape[1] - HEAD :]
    late_low = jnp.concatenate([low[:HALF], far_low, low[HALF:]], axis=0)
    rights = [
        [jnp.concatenate([item[:, block * RANK : (block + 1) * RANK]] * 4, axis=1) for block in range(3)]
        for item in (low, late_low)
    ]
    order_copy.wait()
    for block in range(3):
        for slot in range(SHIFTED):
            lanes = narrow_lanes(slot, block)
            sums_ref[lanes_of(order_ref, SHIFTED + slot, block), :] = dot_first(plain_ref[:, lanes], rights[0][block])
            left = jnp.concatenate([late_ref[:, lanes], half_ref[:, lanes]], axis=0)
            sums_ref[lanes_of(order_ref, slot, block), :] = dot_first(left, rights[1][block])


def up_kernel(*refs):
    source_ref, parts, half_ref, low_ref = refs[0], (refs[1:4], refs[4:7]), refs[7], refs[8]
    out_ref, sums_ref, order_ref, order_sem = refs[9:]
    order_copy = fetch(source_ref, order_ref, order_sem)
    for core in range(C):

        @pl.when(lax.axis_index("c") == core)
        def _():
            accumulate(order_ref, order_copy, *parts[core], half_ref, low_ref, sums_ref)

    place = lax.broadcasted_iota(jnp.int32, (8, HEAD), 1) // RANK
    upper = lax.broadcasted_iota(jnp.int32, (8, HEAD), 0) < 4

    def tile(z, g, third):
        start = ((z * G + g) * 3 + third) * 8
        return sums_ref[start : start + 8, :]

    for g in range(G):
        for z in range(0, Z, 2):
            for c in range(C):
                pair = jnp.concatenate([tile(z, g, 2 * c), tile(z + 1, g, 2 * c)], axis=0)
                out_ref[c, g, z * 8 : z * 8 + 16, :] = pair.astype(BF16)
        middle = []
        for low_z in range(BAND):
            merged = tile(low_z, g, 1)
            for quarter in range(1, 4):
                merged = jnp.where(place == quarter, tile(BAND * quarter + low_z, g, 1), merged)
            middle.append(merged)
        swapped = [pltpu.roll(item, 4, 0) for item in middle]
        for c in range(C):
            rows = []
            for even in range(0, BAND, 2):
                if c == 0:
                    rows.append(jnp.where(upper, middle[even], swapped[even + 1]))
                else:
                    rows.append(jnp.where(upper, swapped[even], middle[even + 1]))
            out_ref[c, g, Z * 8 :, :] = jnp.concatenate(rows, axis=0).astype(BF16)


def down_kernel(normed_ref, first_ref, later_ref, outer_ref, inner_ref, up_ref, mine_ref, other_ref):
    own = lax.axis_index("c")
    total = jnp.where(own == 0, first_ref[...], later_ref[...])
    back = jnp.where(own == 0, inner_ref[...], outer_ref[...])
    total = jnp.concatenate([total[:HALF], total[HALF:] + back], axis=0).astype(BF16)
    lane = lax.broadcasted_iota(jnp.int32, (16, HEAD), 1)
    for z in range(0, Z, 2):
        part = dot_first(normed_ref[:, z * G * 16 : (z + 2) * G * 16], total)
        part = part.reshape(2, G, C, 8, HEAD)
        for g in range(G):
            pieces = []
            for c in range(C):
                down = jnp.concatenate([part[0, g, c], part[1, g, c]], axis=0)
                up = up_ref[c, g, z * 8 : z * 8 + 16, :]
                pieces.append(jnp.where(lane < 3 * RANK, down, up.astype(F32)).astype(BF16))
            start = g * PART + z * 8
            mine_ref[start : start + 16, :] = jnp.where(own == 0, pieces[0], pieces[1])
            other_ref[start : start + 16, :] = jnp.where(own == 0, pieces[1], pieces[0])
    for g in range(G):
        span = slice(g * PART + Z * 8, (g + 1) * PART)
        pieces = [up_ref[c, g, Z * 8 :, :] for c in range(C)]
        mine_ref[span, :] = jnp.where(own == 0, pieces[0], pieces[1])
        other_ref[span, :] = jnp.where(own == 0, pieces[1], pieces[0])


def middle_kernel(come_ref, out_ref):
    total = come_ref[0].astype(F32)
    for item in range(1, G):
        total = total + come_ref[item].astype(F32)
    for z in range(Z):
        start = Z * 8 + z % BAND // 2 * 8
        tiles = jnp.concatenate([total[z * 8 : z * 8 + 8], total[start : start + 8]], axis=0)
        out_ref[z] = tiles.astype(BF16)


def last_kernel(come_ref, down_ref, up_ref):
    c, z = lax.axis_index("c"), lax.axis_index(FAR)
    total = come_ref[0].astype(F32)
    for item in range(1, Z):
        total = total + come_ref[item].astype(F32)
    total = total * ADAPTER_SCALE
    upper, lower = total[:8], total[8:]
    down_ref[...] = upper[:, : 3 * RANK].astype(BF16)
    lower = pltpu.roll(lower, (3 - z // BAND) * RANK, 1)
    moved = lax.rem(z, 2) != c
    lower = jnp.where(moved, pltpu.roll(lower, 4, 0), lower)
    both = jnp.concatenate([upper, lower], axis=0)
    both = jnp.where(c == 1, pltpu.roll(both, 4, 0), both)
    up_ref[...] = both[:12, 3 * RANK :].astype(BF16)


def shape(dims, kind=BF16):
    return jax.ShapeDtypeStruct(dims, kind)


PAIR = (pltpu.VMEM((2, HALF, WIDTH), BF16), pltpu.SemaphoreType.DMA((2,)), *ORDER)


def outer_call(order, keys, values):
    return call(
        outer_kernel,
        "outer_parts",
        shape((HALF, 2 * SHIFTED * HEAD)),
        [ANY, HBM, HBM],
        1_000_000,
        1_000_000,
        limit=53,
        scratch_shapes=PAIR,
    )(order, keys, values)


def inner_call(order, keys, values, normed, down):
    return call(
        inner_kernel,
        "inner_parts",
        (shape((HALF, (2 * SHIFTED + 1) * HEAD)), shape((ROWS, HEAD)), shape((HALF, HEAD))),
        [ANY] + [HBM] * 4,
        130_000_000,
        3_000_000,
        limit=53,
        scratch_shapes=[
            pltpu.VMEM(normed.shape, BF16),
            pltpu.VMEM(down.shape, BF16),
            pltpu.SemaphoreType.DMA((2, WIDE)),
            *PAIR,
        ],
    )(order, keys, values, normed, down)


PLAIN = (shape((ROWS, 3 * NARROW)), shape((ROWS, HEAD), F32))
HALVES = (shape((HALF, 3 * NARROW)), shape((HALF, HEAD), F32))
JOINT = (shape((ROWS, 3 * NARROW)), shape((ROWS, HEAD), F32), shape((HALF, HEAD), F32))


def work_call(body, name, out_shape, inputs, flops, scratch=()):
    return call(
        body,
        name,
        out_shape,
        [ANY] + [VMEM] * (len(inputs) - 1),
        flops,
        6_000_000,
        scratch_shapes=[*scratch, *ORDER],
    )(*inputs)


def down_call(*inputs):
    return call(
        down_kernel,
        "down_gradient",
        (shape((G * PART, HEAD)), shape((G * PART, HEAD))),
        [VMEM] * 6,
        500_000_000,
        4_000_000,
    )(*inputs)


def middle_call(come):
    return call(middle_kernel, "middle_sum", shape((Z, 16, HEAD)), [VMEM], 1_000_000, 600_000)(come)


def last_call(come):
    return call(last_kernel, "last_sum", (shape((8, 3 * RANK)), shape((12, RANK))), [VMEM], 100_000, 70_000)(come)


def per_device(normed, queries, keys, values, cotangent, down, up, order):
    normed, queries, keys, values, cotangent = (
        item[0] for item in (normed, queries, keys, values, cotangent)
    )
    ring = ("yh", "x", "c")
    count = 16
    ahead = [(item, (item + 1) % count) for item in range(count)]
    behind = [(item, (item - 1) % count) for item in range(count)]
    inputs = (order, queries, keys, values, cotangent)
    outer = lax.ppermute(outer_call(order, keys, values), ring, ahead[1::2])
    send, low, far = inner_call(order, keys, values, normed, down.T)
    inner = lax.ppermute(send, ring, ahead[::2])
    outer_low = lax.ppermute(far, ring, ahead[1::2])
    half, half_proj, plain, plain_proj = work_call(
        own_kernel, "own_attention", HALVES + PLAIN, (*inputs, up), 2_000_000_000
    )
    late, proj, back = work_call(
        joint_kernel, "joint_attention", JOINT, (*inputs, outer, up, plain_proj, half_proj), 1_000_000_000
    )
    outer_back = lax.ppermute(back, ring, behind[::2])
    later = work_call(
        later_kernel,
        "later_attention",
        PLAIN[:1] + JOINT,
        (*inputs, inner, up, half_proj, back),
        3_000_000_000,
        [pltpu.VMEM(PLAIN[1].shape, F32)],
    )
    inner_back = lax.ppermute(later[3], ring, behind[1::2])
    up_part = work_call(
        up_kernel,
        "up_gradient",
        shape((C, G, PART, HEAD)),
        (order, plain, late, outer_low, later[0], later[1], inner, half, low),
        1_000_000_000,
        [pltpu.VMEM((3 * WIDTH, HEAD), F32)],
    )
    mine, other = down_call(normed, proj, later[2], outer_back, inner_back, up_part)
    other = lax.ppermute(other, "c", [(0, 1), (1, 0)])
    chip = (mine.astype(F32) + other.astype(F32)).astype(BF16)
    plane = lax.all_to_all(chip.reshape(G, PART, HEAD), NEAR, 0, 0)
    line = lax.all_to_all(middle_call(plane), FAR, 0, 0)
    down_grad, up_grad = last_call(line)
    return down_grad, up_grad.T


def solution(mesh):
    fine = Mesh(mesh.devices.reshape(16, 2, 2, 4, 2), ("z", "yl", "yh", "x", "c"))
    dp, seq = ("z", "yl"), ("yh", "x", "c")
    tokens = P(dp, seq, None)
    in_specs = (tokens,) * 5 + (P(),) * 3
    out_specs = (P(dp + seq, None), P(None, dp + seq))
    return jax.shard_map(per_device, mesh=fine, in_specs=in_specs, out_specs=out_specs, check_vma=False)
```

```python
import jax
import jax.numpy as jnp
from jax import lax
from jax.experimental import pallas as pl
from jax.experimental.pallas import tpu as pltpu
from jax.sharding import Mesh
from jax.sharding import PartitionSpec as P

HEAD = 128
ROWS = 160
HALF = 80
HEADS = 16
SHIFTED = 8
WIDTH = HEADS * HEAD
MODEL = 4096
RANK = 32
SCALE = HEAD ** -0.5
ADAPTER_SCALE = 0.25
NEAR, FAR = ("yl", "yh", "x"), ("z",)
Z, G, C = 16, 16, 2
BAND = Z // 4
WIDE = 2
NARROW = SHIFTED * HEAD
PART = Z * 8 + BAND * 4

BF16, F32 = jnp.bfloat16, jnp.float32
VMEM = pl.BlockSpec(memory_space=pltpu.VMEM)
HBM = pl.BlockSpec(memory_space=pltpu.HBM)
ANY = pl.BlockSpec(memory_space=pl.ANY)
ORDER = (pltpu.SMEM((HEADS,), jnp.int32), pltpu.SemaphoreType.DMA)


def call(body, name, out_shape, in_specs, flops, size, limit=32, out_specs=None, **rest):
    return pl.pallas_call(
        body,
        name=name,
        out_shape=out_shape,
        in_specs=in_specs,
        out_specs=out_specs or jax.tree.map(lambda _: VMEM, out_shape),
        compiler_params=pltpu.CompilerParams(vmem_limit_bytes=limit * 1024 * 1024),
        cost_estimate=pl.CostEstimate(flops=flops, bytes_accessed=size, transcendentals=0),
        **rest,
    )


def dot(left, right):
    return jnp.dot(left, right, preferred_element_type=F32)


def dot_last(left, right):
    return lax.dot_general(left, right, (((1,), (1,)), ((), ())), preferred_element_type=F32)


def dot_first(left, right):
    return lax.dot_general(left, right, (((0,), (0,)), ((), ())), preferred_element_type=F32)


def scores_of(parts, allowed):
    queries, keys, values, cotangents = zip(*parts)
    scores = [jnp.where(allowed, dot_last(key, query), -jnp.inf) for query, key in zip(queries, keys)]
    dprobs = [dot_last(value, cotangent) for value, cotangent in zip(values, cotangents)]
    tops = [jnp.max(item, axis=0, keepdims=True) for item in scores]
    powers = [jnp.exp((item - top) * SCALE) for item, top in zip(scores, tops)]
    probs = [item * (1.0 / jnp.sum(item, axis=0, keepdims=True)) for item in powers]
    weights = [item.astype(BF16) for item in probs]
    deltas = [
        jnp.sum(weight.astype(F32) * dprob, axis=0, keepdims=True) for weight, dprob in zip(weights, dprobs)
    ]
    dscores = [
        (prob * (dprob - delta)).astype(BF16) for prob, dprob, delta in zip(probs, dprobs, deltas)
    ]
    return weights, dscores


def attend(parts, allowed):
    queries, keys, _, cotangents = zip(*parts)
    weights, dscores = scores_of(parts, allowed)
    dvalues = [dot(weight, cotangent).astype(BF16) for weight, cotangent in zip(weights, cotangents)]
    dkeys = [(dot(dscore, query) * SCALE).astype(BF16) for dscore, query in zip(dscores, queries)]
    dqueries = [(dot_first(dscore, key) * SCALE).astype(BF16) for dscore, key in zip(dscores, keys)]
    return list(zip(dqueries, dkeys, dvalues))


def causal(keys, queries, ahead):
    row = lax.broadcasted_iota(jnp.int32, (keys, queries), 0)
    column = lax.broadcasted_iota(jnp.int32, (keys, queries), 1)
    return row <= column + ahead


def lanes_of(order_ref, slot, block=0):
    return pl.ds(pl.multiple_of(order_ref[slot] * HEAD + block * WIDTH, HEAD), HEAD)


def scalars(ref):
    lane = lax.broadcasted_iota(jnp.int32, (1, HEADS), 1)
    return [ref[0, slot] for slot in range(HEADS)]


def narrow_lanes(slot, block=0):
    return slice(block * NARROW + slot * HEAD, block * NARROW + (slot + 1) * HEAD)


def fetch(source_ref, order_ref, sem):
    copy = pltpu.make_async_copy(source_ref, order_ref, sem)
    copy.start()
    return copy


def start_low(normed_ref, down_ref, normed_own, down_own, wide_sems, rows):
    copies = []
    span = MODEL // WIDE
    for part in range(WIDE):
        lanes = slice(part * span, (part + 1) * span)
        copies.append(fetch(normed_ref.at[rows, lanes], normed_own.at[rows, lanes], wide_sems.at[0, part]))
        copies.append(fetch(down_ref.at[:, lanes], down_own.at[:, lanes], wide_sems.at[1, part]))
    return copies


def finish_low(copies, normed_own, down_own, rows):
    low = None
    span = MODEL // WIDE
    for part in range(WIDE):
        lanes = slice(part * span, (part + 1) * span)
        for copy in copies[2 * part : 2 * part + 2]:
            copy.wait()
        term = dot_last(normed_own[rows, lanes], down_own[:, lanes])
        low = term if low is None else low + term
    low = low.astype(BF16)
    return jnp.concatenate([low, jnp.zeros((low.shape[0], HEAD - 3 * RANK), BF16)], axis=1)


def prepare(
    rows,
    source_ref,
    key_ref,
    value_ref,
    normed_ref,
    down_ref,
    send_ref,
    low_ref,
    pair_own,
    normed_own,
    down_own,
    pair_sems,
    wide_sems,
    order_ref,
    order_sem,
):
    order_copy = fetch(source_ref, order_ref, order_sem)
    pair_copies = [
        fetch(source.at[HALF:], pair_own.at[item], pair_sems.at[item])
        for item, source in enumerate((key_ref, value_ref))
    ]
    wide_copies = start_low(normed_ref, down_ref, normed_own, down_own, wide_sems, rows)
    order_copy.wait()
    for item in range(2):
        pair_copies[item].wait()
        for slot in range(SHIFTED):
            place = item * SHIFTED + slot
            send_ref[:, place * HEAD : (place + 1) * HEAD] = pair_own[item, :, lanes_of(order_ref, slot)]
    low = finish_low(wide_copies, normed_own, down_own, rows)
    low_ref[...] = low
    send_ref[:, 2 * SHIFTED * HEAD :] = low[low.shape[0] - HALF :]


def outer_kernel(*refs):
    @pl.when(lax.axis_index("c") == 1)
    def _():
        prepare(slice(HALF, ROWS), *refs)


def inner_kernel(tail_ref, *refs):
    core = lax.axis_index("c")

    @pl.when(core == 0)
    def _():
        prepare(slice(0, ROWS), *refs)

    @pl.when(core == 1)
    def _():
        normed_ref, down_ref, low_ref = refs[3], refs[4], refs[6]
        normed_own, down_own, wide_sems = refs[8], refs[9], refs[11]
        rows = slice(0, HALF)
        copies = start_low(normed_ref, down_ref, normed_own, down_own, wide_sems, rows)
        low_ref[:HALF, :] = finish_low(copies, normed_own, down_own, rows)
        low_ref[HALF:, :] = tail_ref[...]


def project(order_ref, grads_ref, up_ref, slots, blocks=range(3), rows=slice(None)):
    total = None
    for block in blocks:
        up = jnp.concatenate([up_ref[:, lanes_of(order_ref, slot, block)] for slot in slots], axis=1)
        parts = [up if place == block else jnp.zeros_like(up) for place in range(4)]
        columns = slice(block * NARROW, (block + 1) * NARROW)
        term = dot_last(grads_ref[rows, columns], jnp.concatenate(parts, axis=0))
        total = term if total is None else total + term
    return total


def half_work(order_ref, refs, up_ref, half_ref, half_proj_ref):
    slots = range(SHIFTED)
    parts = [[ref[HALF:, lanes_of(order_ref, slot)] for ref in refs] for slot in slots]
    for slot, grads in zip(slots, attend(parts, causal(HALF, HALF, 0))):
        for block in range(3):
            half_ref[:, narrow_lanes(slot, block)] = grads[block]
    half_proj_ref[...] = project(order_ref, half_ref, up_ref, slots)


def plain_work(order_ref, refs, up_ref, plain_ref, plain_proj_ref):
    slots = range(SHIFTED, HEADS)
    parts = [[ref[:, lanes_of(order_ref, slot)] for ref in refs] for slot in slots]
    for slot, grads in zip(slots, attend(parts, causal(ROWS, ROWS, 0))):
        for block in range(3):
            plain_ref[:, narrow_lanes(slot - SHIFTED, block)] = grads[block]
    plain_proj_ref[...] = project(order_ref, plain_ref, up_ref, slots)


def joint_work(order_ref, refs, come_ref, up_ref, late_ref, back_ref, far_ref, dscore_ref):
    query_ref, key_ref, value_ref, cot_ref = refs
    far_ref[...] = come_ref[:, 2 * SHIFTED * HEAD :]
    slots = range(SHIFTED)
    parts = []
    for slot in slots:
        lanes = lanes_of(order_ref, slot)
        key, value = (
            jnp.concatenate([come_ref[:, place * HEAD : (place + 1) * HEAD], ref[:HALF, lanes]], axis=0)
            for place, ref in ((slot, key_ref), (SHIFTED + slot, value_ref))
        )
        parts.append([query_ref[:HALF, lanes], key, value, cot_ref[:HALF, lanes]])
    weights, dscores = scores_of(parts, causal(ROWS, HALF, HALF))
    for slot, (query, _, _, cotangent) in zip(slots, parts):
        dscore_ref[slot] = dscores[slot]
        for block, grad in ((1, dot(dscores[slot], query) * SCALE), (2, dot(weights[slot], cotangent))):
            grad = grad.astype(BF16)
            late_ref[:HALF, narrow_lanes(slot, block)] = grad[HALF:]
            late_ref[HALF:, narrow_lanes(slot, block)] = grad[:HALF]
    back_ref[...] = project(order_ref, late_ref, up_ref, slots, (1, 2), slice(HALF, ROWS))


def rest_work(
    order_ref, key_ref, come_ref, up_ref, late_ref, dscore_ref, plain_proj_ref, half_proj_ref, dquery_ref, proj_ref
):
    slots = range(SHIFTED)
    for slot in slots:
        far_key = come_ref[:, slot * HEAD : (slot + 1) * HEAD]
        key = jnp.concatenate([far_key, key_ref[:HALF, lanes_of(order_ref, slot)]], axis=0)
        dquery_ref[:, narrow_lanes(slot)] = (dot_first(dscore_ref[slot], key) * SCALE).astype(BF16)
    total = project(order_ref, late_ref, up_ref, slots, (1, 2), slice(0, HALF))
    total = total + project(order_ref, dquery_ref, up_ref, slots, (0,))
    plain = plain_proj_ref[...]
    proj_ref[...] = jnp.concatenate([plain[:HALF] + total, plain[HALF:] + half_proj_ref[...]], axis=0)


def own_kernel(*refs):
    source_ref, inputs, up_ref = refs[0], refs[1:5], refs[5]
    half_refs, plain_refs = refs[6:8], refs[8:10]
    order_ref = scalars(source_ref)

    @pl.when(lax.axis_index("c") == 0)
    def _():
        plain_work(order_ref, inputs, up_ref, *plain_refs)

    half_work(order_ref, inputs, up_ref, *half_refs)


def joint_kernel(*refs):
    source_ref, inputs, rest = refs[0], refs[1:5], refs[5:]

    @pl.when(lax.axis_index("c") == 0)
    def _():
        joint_work(scalars(source_ref), inputs, *rest)


def rest_kernel(source_ref, *refs):
    @pl.when(lax.axis_index("c") == 0)
    def _():
        rest_work(scalars(source_ref), *refs)


def later_kernel(*refs):
    source_ref, inputs, come_ref, up_ref, half_proj_ref = refs[0], refs[1:5], refs[5], refs[6], refs[7]
    plain_ref, late_ref, back_ref, far_ref, dquery_ref, proj_ref, plain_proj_ref, dscore_ref = refs[9:]

    @pl.when(lax.axis_index("c") == 1)
    def _():
        order_ref = scalars(source_ref)
        plain_work(order_ref, inputs, up_ref, plain_ref, plain_proj_ref)
        joint_work(order_ref, inputs, come_ref, up_ref, late_ref, back_ref, far_ref, dscore_ref)
        rest_work(
            order_ref,
            inputs[1],
            come_ref,
            up_ref,
            late_ref,
            dscore_ref,
            plain_proj_ref,
            half_proj_ref,
            dquery_ref,
            proj_ref,
        )


def accumulate(order_ref, plain_ref, late_ref, far_ref, dquery_ref, half_ref, low_ref, sums_ref):
    low = low_ref[...]
    late_low = jnp.concatenate([low, far_ref[...]], axis=0)
    rights = [
        [jnp.concatenate([item[:, block * RANK : (block + 1) * RANK]] * 4, axis=1) for block in range(3)]
        for item in (low, late_low)
    ]
    for block in range(3):
        for slot in range(SHIFTED):
            lanes = narrow_lanes(slot, block)
            sums_ref[lanes_of(order_ref, SHIFTED + slot, block), :] = dot_first(plain_ref[:, lanes], rights[0][block])
            first = late_ref[:HALF, lanes] if block else dquery_ref[:, lanes]
            left = [first, half_ref[:, lanes]] + [late_ref[HALF:, lanes]] * (block > 0)
            right = rights[1 if block else 0][block]
            sums_ref[lanes_of(order_ref, slot, block), :] = dot_first(jnp.concatenate(left, axis=0), right)


def up_kernel(*refs):
    source_ref, parts, half_ref, low_ref = refs[0], (refs[1:5], refs[5:9]), refs[9], refs[10]
    out_ref, sums_ref = refs[11:]
    order_ref = scalars(source_ref)
    for core in range(C):

        @pl.when(lax.axis_index("c") == core)
        def _():
            accumulate(order_ref, *parts[core], half_ref, low_ref, sums_ref)

    place = lax.broadcasted_iota(jnp.int32, (8, HEAD), 1) // RANK
    upper = lax.broadcasted_iota(jnp.int32, (8, HEAD), 0) < 4

    def tile(z, g, third):
        start = ((z * G + g) * 3 + third) * 8
        return sums_ref[start : start + 8, :]

    for g in range(G):
        for z in range(0, Z, 2):
            for c in range(C):
                pair = jnp.concatenate([tile(z, g, 2 * c), tile(z + 1, g, 2 * c)], axis=0)
                out_ref[c, g, z * 8 : z * 8 + 16, :] = pair.astype(BF16)
        middle = []
        for low_z in range(BAND):
            merged = tile(low_z, g, 1)
            for quarter in range(1, 4):
                merged = jnp.where(place == quarter, tile(BAND * quarter + low_z, g, 1), merged)
            middle.append(merged)
        swapped = [pltpu.roll(item, 4, 0) for item in middle]
        for c in range(C):
            rows = []
            for even in range(0, BAND, 2):
                if c == 0:
                    rows.append(jnp.where(upper, middle[even], swapped[even + 1]))
                else:
                    rows.append(jnp.where(upper, swapped[even], middle[even + 1]))
            out_ref[c, g, Z * 8 :, :] = jnp.concatenate(rows, axis=0).astype(BF16)


def down_kernel(normed_ref, first_ref, later_ref, outer_ref, inner_ref, up_ref, mine_ref, other_ref):
    own = lax.axis_index("c")
    total = jnp.where(own == 0, first_ref[...], later_ref[...])
    back = jnp.where(own == 0, inner_ref[...], outer_ref[...])
    total = jnp.concatenate([total[:HALF], total[HALF:] + back], axis=0).astype(BF16)
    lane = lax.broadcasted_iota(jnp.int32, (16, HEAD), 1)
    for z in range(0, Z, 2):
        part = dot_first(normed_ref[:, z * G * 16 : (z + 2) * G * 16], total)
        part = part.reshape(2, G, C, 8, HEAD)
        for g in range(G):
            pieces = []
            for c in range(C):
                down = jnp.concatenate([part[0, g, c], part[1, g, c]], axis=0)
                up = up_ref[c, g, z * 8 : z * 8 + 16, :]
                pieces.append(jnp.where(lane < 3 * RANK, down, up.astype(F32)).astype(BF16))
            start = g * PART + z * 8
            mine_ref[start : start + 16, :] = jnp.where(own == 0, pieces[0], pieces[1])
            other_ref[start : start + 16, :] = jnp.where(own == 0, pieces[1], pieces[0])
    for g in range(G):
        span = slice(g * PART + Z * 8, (g + 1) * PART)
        pieces = [up_ref[c, g, Z * 8 :, :] for c in range(C)]
        mine_ref[span, :] = jnp.where(own == 0, pieces[0], pieces[1])
        other_ref[span, :] = jnp.where(own == 0, pieces[1], pieces[0])


def middle_kernel(come_ref, out_ref):
    total = come_ref[0].astype(F32)
    for item in range(1, G):
        total = total + come_ref[item].astype(F32)
    for z in range(Z):
        start = Z * 8 + z % BAND // 2 * 8
        tiles = jnp.concatenate([total[z * 8 : z * 8 + 8], total[start : start + 8]], axis=0)
        out_ref[z] = tiles.astype(BF16)


def last_kernel(come_ref, down_ref, up_ref):
    c, z = lax.axis_index("c"), lax.axis_index(FAR)
    total = come_ref[0].astype(F32)
    for item in range(1, Z):
        total = total + come_ref[item].astype(F32)
    total = total * ADAPTER_SCALE
    upper, lower = total[:8], total[8:]
    down_ref[...] = upper[:, : 3 * RANK].astype(BF16)
    lower = pltpu.roll(lower, (3 - z // BAND) * RANK, 1)
    moved = lax.rem(z, 2) != c
    lower = jnp.where(moved, pltpu.roll(lower, 4, 0), lower)
    both = jnp.concatenate([upper, lower], axis=0)
    both = jnp.where(c == 1, pltpu.roll(both, 4, 0), both)
    up_ref[...] = both[:12, 3 * RANK :].astype(BF16)


def shape(dims, kind=BF16):
    return jax.ShapeDtypeStruct(dims, kind)


def prepare_call(body, name, rows, extra, order, keys, values, normed, down):
    return call(
        body,
        name,
        (shape((HALF, (2 * SHIFTED + 1) * HEAD)), shape((rows, HEAD))),
        [VMEM] * len(extra) + [ANY] + [HBM] * 4,
        130_000_000,
        3_000_000,
        limit=53,
        scratch_shapes=[
            pltpu.VMEM((2, HALF, WIDTH), BF16),
            pltpu.VMEM(normed.shape, BF16),
            pltpu.VMEM(down.shape, BF16),
            pltpu.SemaphoreType.DMA((2,)),
            pltpu.SemaphoreType.DMA((2, WIDE)),
            *ORDER,
        ],
    )(*extra, order, keys, values, normed, down)


PLAIN = (shape((ROWS, 3 * NARROW)), shape((ROWS, HEAD), F32))
HALVES = (shape((HALF, 3 * NARROW)), shape((HALF, HEAD), F32))
JOINT = (shape((ROWS, 3 * NARROW)), shape((HALF, HEAD), F32), shape((HALF, HEAD)))
DSCORE = (SHIFTED, ROWS, HALF)
REST = (shape((HALF, NARROW)), shape((ROWS, HEAD), F32))


def work_call(body, name, out_shape, inputs, flops, scratch=()):
    return call(
        body,
        name,
        out_shape,
        [VMEM] * len(inputs),
        flops,
        6_000_000,
        scratch_shapes=scratch,
    )(*inputs)


def down_call(*inputs):
    return call(
        down_kernel,
        "down_gradient",
        (shape((G * PART, HEAD)), shape((G * PART, HEAD))),
        [VMEM] * 6,
        500_000_000,
        4_000_000,
    )(*inputs)


def middle_call(come):
    return call(middle_kernel, "middle_sum", shape((Z, 16, HEAD)), [VMEM], 1_000_000, 600_000)(come)


def last_call(come):
    return call(last_kernel, "last_sum", (shape((8, 3 * RANK)), shape((12, RANK))), [VMEM], 100_000, 70_000)(come)


def per_device(normed, queries, keys, values, cotangent, down, up, order):
    normed, queries, keys, values, cotangent = (
        item[0] for item in (normed, queries, keys, values, cotangent)
    )
    ring = ("yh", "x", "c")
    count = 16
    ahead = [(item, (item + 1) % count) for item in range(count)]
    behind = [(item, (item - 1) % count) for item in range(count)]
    sources = (order, keys, values, normed, down.T)
    order = order.reshape(1, HEADS)
    inputs = (order, queries, keys, values, cotangent)
    send, tail = prepare_call(outer_kernel, "outer_parts", HALF, (), *sources)
    outer = lax.ppermute(send, ring, ahead[1::2])
    send, low = prepare_call(inner_kernel, "inner_parts", ROWS, (tail,), *sources)
    inner = lax.ppermute(send, ring, ahead[::2])
    half, half_proj, plain, plain_proj = work_call(
        own_kernel, "own_attention", HALVES + PLAIN, (*inputs, up), 2_000_000_000
    )
    late, back, far, dscore = work_call(
        joint_kernel, "joint_attention", (*JOINT, shape(DSCORE)), (*inputs, outer, up), 1_000_000_000
    )
    outer_back = lax.ppermute(back, ring, behind[::2])
    dquery, proj = work_call(
        rest_kernel, "rest_attention", REST, (order, keys, outer, up, late, dscore, plain_proj, half_proj), 500_000_000
    )
    later = work_call(
        later_kernel,
        "later_attention",
        PLAIN[:1] + JOINT + REST,
        (*inputs, inner, up, half_proj, far),
        3_000_000_000,
        [pltpu.VMEM(PLAIN[1].shape, F32), pltpu.VMEM(DSCORE, BF16)],
    )
    inner_back = lax.ppermute(later[2], ring, behind[1::2])
    up_part = work_call(
        up_kernel,
        "up_gradient",
        shape((C, G, PART, HEAD)),
        (order, plain, late, far, dquery, later[0], later[1], later[3], later[4], half, low),
        1_000_000_000,
        [pltpu.VMEM((3 * WIDTH, HEAD), F32)],
    )
    mine, other = down_call(normed, proj, later[5], outer_back, inner_back, up_part)
    other = lax.ppermute(other, "c", [(0, 1), (1, 0)])
    chip = (mine.astype(F32) + other.astype(F32)).astype(BF16)
    plane = lax.all_to_all(chip.reshape(G, PART, HEAD), NEAR, 0, 0)
    line = lax.all_to_all(middle_call(plane), FAR, 0, 0)
    down_grad, up_grad = last_call(line)
    return down_grad, up_grad.T


def solution(mesh):
    fine = Mesh(mesh.devices.reshape(16, 2, 2, 4, 2), ("z", "yl", "yh", "x", "c"))
    dp, seq = ("z", "yl"), ("yh", "x", "c")
    tokens = P(dp, seq, None)
    in_specs = (tokens,) * 5 + (P(),) * 3
    out_specs = (P(dp + seq, None), P(None, dp + seq))
    return jax.shard_map(per_device, mesh=fine, in_specs=in_specs, out_specs=out_specs, check_vma=False)
```

```python
import jax
import jax.numpy as jnp
from jax import lax
from jax.experimental import pallas as pl
from jax.experimental.pallas import tpu as pltpu
from jax.sharding import Mesh
from jax.sharding import PartitionSpec as P

HEAD = 128
ROWS = 160
HALF = 80
HEADS = 16
SHIFTED = 8
WIDTH = HEADS * HEAD
MODEL = 4096
RANK = 32
SCALE = HEAD ** -0.5
ADAPTER_SCALE = 0.25
NEAR, FAR = ("yl", "yh", "x"), ("z",)
Z, G, C = 16, 16, 2
BAND = Z // 4
WIDE = 2
NARROW = SHIFTED * HEAD
PART = Z * 8 + BAND * 4

BF16, F32 = jnp.bfloat16, jnp.float32
VMEM = pl.BlockSpec(memory_space=pltpu.VMEM)
HBM = pl.BlockSpec(memory_space=pltpu.HBM)
ANY = pl.BlockSpec(memory_space=pl.ANY)
ORDER = (pltpu.SMEM((HEADS,), jnp.int32), pltpu.SemaphoreType.DMA)


def call(body, name, out_shape, in_specs, flops, size, limit=32, out_specs=None, **rest):
    return pl.pallas_call(
        body,
        name=name,
        out_shape=out_shape,
        in_specs=in_specs,
        out_specs=out_specs or jax.tree.map(lambda _: VMEM, out_shape),
        compiler_params=pltpu.CompilerParams(vmem_limit_bytes=limit * 1024 * 1024),
        cost_estimate=pl.CostEstimate(flops=flops, bytes_accessed=size, transcendentals=0),
        **rest,
    )


def dot(left, right):
    return jnp.dot(left, right, preferred_element_type=F32)


def dot_last(left, right):
    return lax.dot_general(left, right, (((1,), (1,)), ((), ())), preferred_element_type=F32)


def dot_first(left, right):
    return lax.dot_general(left, right, (((0,), (0,)), ((), ())), preferred_element_type=F32)


def scores_of(parts, allowed):
    queries, keys, values, cotangents = zip(*parts)
    scores = [jnp.where(allowed, dot_last(key, query), -jnp.inf) for query, key in zip(queries, keys)]
    dprobs = [dot_last(value, cotangent) for value, cotangent in zip(values, cotangents)]
    tops = [jnp.max(item, axis=0, keepdims=True) for item in scores]
    powers = [jnp.exp((item - top) * SCALE) for item, top in zip(scores, tops)]
    probs = [item * (1.0 / jnp.sum(item, axis=0, keepdims=True)) for item in powers]
    weights = [item.astype(BF16) for item in probs]
    deltas = [
        jnp.sum(weight.astype(F32) * dprob, axis=0, keepdims=True) for weight, dprob in zip(weights, dprobs)
    ]
    dscores = [
        (prob * (dprob - delta)).astype(BF16) for prob, dprob, delta in zip(probs, dprobs, deltas)
    ]
    return weights, dscores


def attend(parts, allowed):
    queries, keys, _, cotangents = zip(*parts)
    weights, dscores = scores_of(parts, allowed)
    dvalues = [dot(weight, cotangent).astype(BF16) for weight, cotangent in zip(weights, cotangents)]
    dkeys = [(dot(dscore, query) * SCALE).astype(BF16) for dscore, query in zip(dscores, queries)]
    dqueries = [(dot_first(dscore, key) * SCALE).astype(BF16) for dscore, key in zip(dscores, keys)]
    return list(zip(dqueries, dkeys, dvalues))


def causal(keys, queries, ahead):
    row = lax.broadcasted_iota(jnp.int32, (keys, queries), 0)
    column = lax.broadcasted_iota(jnp.int32, (keys, queries), 1)
    return row <= column + ahead


def lanes_of(order_ref, slot, block=0):
    return pl.ds(pl.multiple_of(order_ref[slot] * HEAD + block * WIDTH, HEAD), HEAD)


def scalars(ref):
    lane = lax.broadcasted_iota(jnp.int32, (1, HEADS), 1)
    return [ref[0, slot] for slot in range(HEADS)]


def narrow_lanes(slot, block=0):
    return slice(block * NARROW + slot * HEAD, block * NARROW + (slot + 1) * HEAD)


def fetch(source_ref, order_ref, sem):
    copy = pltpu.make_async_copy(source_ref, order_ref, sem)
    copy.start()
    return copy


def start_low(normed_ref, down_ref, normed_own, down_own, wide_sems, rows):
    copies = []
    span = MODEL // WIDE
    for part in range(WIDE):
        lanes = slice(part * span, (part + 1) * span)
        copies.append(fetch(normed_ref.at[rows, lanes], normed_own.at[rows, lanes], wide_sems.at[0, part]))
        copies.append(fetch(down_ref.at[:, lanes], down_own.at[:, lanes], wide_sems.at[1, part]))
    return copies


def finish_low(copies, normed_own, down_own, rows):
    low = None
    span = MODEL // WIDE
    for part in range(WIDE):
        lanes = slice(part * span, (part + 1) * span)
        for copy in copies[2 * part : 2 * part + 2]:
            copy.wait()
        term = dot_last(normed_own[rows, lanes], down_own[:, lanes])
        low = term if low is None else low + term
    low = low.astype(BF16)
    return jnp.concatenate([low, jnp.zeros((low.shape[0], HEAD - 3 * RANK), BF16)], axis=1)


def prepare(
    rows,
    source_ref,
    key_ref,
    value_ref,
    normed_ref,
    down_ref,
    send_ref,
    low_ref,
    pair_own,
    normed_own,
    down_own,
    pair_sems,
    wide_sems,
    order_ref,
    order_sem,
):
    order_copy = fetch(source_ref, order_ref, order_sem)
    pair_copies = [
        fetch(source.at[HALF:], pair_own.at[item], pair_sems.at[item])
        for item, source in enumerate((key_ref, value_ref))
    ]
    wide_copies = start_low(normed_ref, down_ref, normed_own, down_own, wide_sems, rows)
    order_copy.wait()
    for item in range(2):
        pair_copies[item].wait()
        for slot in range(SHIFTED):
            place = item * SHIFTED + slot
            send_ref[:, place * HEAD : (place + 1) * HEAD] = pair_own[item, :, lanes_of(order_ref, slot)]
    low = finish_low(wide_copies, normed_own, down_own, rows)
    low_ref[...] = low
    send_ref[:, 2 * SHIFTED * HEAD :] = low[low.shape[0] - HALF :]


def outer_kernel(*refs):
    @pl.when(lax.axis_index("c") == 1)
    def _():
        prepare(slice(HALF, ROWS), *refs)


def inner_kernel(tail_ref, *refs):
    core = lax.axis_index("c")

    @pl.when(core == 0)
    def _():
        prepare(slice(0, ROWS), *refs)

    @pl.when(core == 1)
    def _():
        normed_ref, down_ref, low_ref = refs[3], refs[4], refs[6]
        normed_own, down_own, wide_sems = refs[8], refs[9], refs[11]
        rows = slice(0, HALF)
        copies = start_low(normed_ref, down_ref, normed_own, down_own, wide_sems, rows)
        low_ref[:HALF, :] = finish_low(copies, normed_own, down_own, rows)
        low_ref[HALF:, :] = tail_ref[...]


def project(order_ref, grads_ref, up_ref, slots, blocks=range(3), rows=slice(None)):
    total = None
    for block in blocks:
        up = jnp.concatenate([up_ref[:, lanes_of(order_ref, slot, block)] for slot in slots], axis=1)
        parts = [up if place == block else jnp.zeros_like(up) for place in range(4)]
        columns = slice(block * NARROW, (block + 1) * NARROW)
        term = dot_last(grads_ref[rows, columns], jnp.concatenate(parts, axis=0))
        total = term if total is None else total + term
    return total


def half_work(order_ref, refs, up_ref, half_ref, half_proj_ref):
    slots = range(SHIFTED)
    parts = [[ref[HALF:, lanes_of(order_ref, slot)] for ref in refs] for slot in slots]
    for slot, grads in zip(slots, attend(parts, causal(HALF, HALF, 0))):
        for block in range(3):
            half_ref[:, narrow_lanes(slot, block)] = grads[block]
    half_proj_ref[...] = project(order_ref, half_ref, up_ref, slots)


def plain_work(order_ref, refs, up_ref, plain_ref, plain_proj_ref):
    slots = range(SHIFTED, HEADS)
    parts = [[ref[:, lanes_of(order_ref, slot)] for ref in refs] for slot in slots]
    for slot, grads in zip(slots, attend(parts, causal(ROWS, ROWS, 0))):
        for block in range(3):
            plain_ref[:, narrow_lanes(slot - SHIFTED, block)] = grads[block]
    plain_proj_ref[...] = project(order_ref, plain_ref, up_ref, slots)


def joint_work(order_ref, refs, come_ref, up_ref, late_ref, back_ref, far_ref, dscore_ref):
    query_ref, key_ref, value_ref, cot_ref = refs
    far_ref[...] = come_ref[:, 2 * SHIFTED * HEAD :]
    slots = range(SHIFTED)
    parts = []
    for slot in slots:
        lanes = lanes_of(order_ref, slot)
        key, value = (
            jnp.concatenate([come_ref[:, place * HEAD : (place + 1) * HEAD], ref[:HALF, lanes]], axis=0)
            for place, ref in ((slot, key_ref), (SHIFTED + slot, value_ref))
        )
        parts.append([query_ref[:HALF, lanes], key, value, cot_ref[:HALF, lanes]])
    weights, dscores = scores_of(parts, causal(ROWS, HALF, HALF))
    for slot, (query, _, _, cotangent) in zip(slots, parts):
        dscore_ref[slot] = dscores[slot]
        for block, grad in ((1, dot(dscores[slot], query) * SCALE), (2, dot(weights[slot], cotangent))):
            grad = grad.astype(BF16)
            late_ref[:HALF, narrow_lanes(slot, block)] = grad[HALF:]
            late_ref[HALF:, narrow_lanes(slot, block)] = grad[:HALF]
    back_ref[...] = project(order_ref, late_ref, up_ref, slots, (1, 2), slice(HALF, ROWS))


def rest_work(
    order_ref, key_ref, come_ref, up_ref, late_ref, dscore_ref, plain_proj_ref, half_proj_ref, dquery_ref, proj_ref
):
    slots = range(SHIFTED)
    for slot in slots:
        far_key = come_ref[:, slot * HEAD : (slot + 1) * HEAD]
        key = jnp.concatenate([far_key, key_ref[:HALF, lanes_of(order_ref, slot)]], axis=0)
        dquery_ref[:, narrow_lanes(slot)] = (dot_first(dscore_ref[slot], key) * SCALE).astype(BF16)
    total = project(order_ref, late_ref, up_ref, slots, (1, 2), slice(0, HALF))
    total = total + project(order_ref, dquery_ref, up_ref, slots, (0,))
    plain = plain_proj_ref[...]
    proj_ref[...] = jnp.concatenate([plain[:HALF] + total, plain[HALF:] + half_proj_ref[...]], axis=0)


def own_kernel(*refs):
    source_ref, inputs, up_ref = refs[0], refs[1:5], refs[5]
    half_refs, plain_refs = refs[6:8], refs[8:10]
    order_ref = scalars(source_ref)

    @pl.when(lax.axis_index("c") == 0)
    def _():
        plain_work(order_ref, inputs, up_ref, *plain_refs)

    half_work(order_ref, inputs, up_ref, *half_refs)


def joint_kernel(*refs):
    source_ref, inputs, rest = refs[0], refs[1:5], refs[5:]

    @pl.when(lax.axis_index("c") == 0)
    def _():
        joint_work(scalars(source_ref), inputs, *rest)


def rest_kernel(source_ref, *refs):
    @pl.when(lax.axis_index("c") == 0)
    def _():
        rest_work(scalars(source_ref), *refs)


def later_kernel(*refs):
    source_ref, inputs, come_ref, up_ref, half_proj_ref = refs[0], refs[1:5], refs[5], refs[6], refs[7]
    plain_ref, late_ref, back_ref, far_ref, dquery_ref, proj_ref, plain_proj_ref, dscore_ref = refs[9:]

    @pl.when(lax.axis_index("c") == 1)
    def _():
        order_ref = scalars(source_ref)
        plain_work(order_ref, inputs, up_ref, plain_ref, plain_proj_ref)
        joint_work(order_ref, inputs, come_ref, up_ref, late_ref, back_ref, far_ref, dscore_ref)
        rest_work(
            order_ref,
            inputs[1],
            come_ref,
            up_ref,
            late_ref,
            dscore_ref,
            plain_proj_ref,
            half_proj_ref,
            dquery_ref,
            proj_ref,
        )


def accumulate(order_ref, plain_ref, late_ref, far_ref, dquery_ref, half_ref, low_ref, sums_ref):
    low = low_ref[...]
    late_low = jnp.concatenate([low, far_ref[...]], axis=0)
    rights = [
        [jnp.concatenate([item[:, block * RANK : (block + 1) * RANK]] * 4, axis=1) for block in range(3)]
        for item in (low, late_low)
    ]
    for block in range(3):
        for slot in range(SHIFTED):
            lanes = narrow_lanes(slot, block)
            sums_ref[lanes_of(order_ref, SHIFTED + slot, block), :] = dot_first(plain_ref[:, lanes], rights[0][block])
            first = late_ref[:HALF, lanes] if block else dquery_ref[:, lanes]
            left = [first, half_ref[:, lanes]] + [late_ref[HALF:, lanes]] * (block > 0)
            right = rights[1 if block else 0][block]
            sums_ref[lanes_of(order_ref, slot, block), :] = dot_first(jnp.concatenate(left, axis=0), right)


def up_kernel(*refs):
    source_ref, parts, half_ref, low_ref = refs[0], (refs[1:5], refs[5:9]), refs[9], refs[10]
    out_ref, sums_ref = refs[11:]
    order_ref = scalars(source_ref)
    for core in range(C):

        @pl.when(lax.axis_index("c") == core)
        def _():
            accumulate(order_ref, *parts[core], half_ref, low_ref, sums_ref)

    place = lax.broadcasted_iota(jnp.int32, (8, HEAD), 1) // RANK
    upper = lax.broadcasted_iota(jnp.int32, (8, HEAD), 0) < 4

    def tile(z, g, third):
        start = ((z * G + g) * 3 + third) * 8
        return sums_ref[start : start + 8, :]

    for g in range(G):
        for z in range(0, Z, 2):
            for c in range(C):
                pair = jnp.concatenate([tile(z, g, 2 * c), tile(z + 1, g, 2 * c)], axis=0)
                out_ref[c, g, z * 8 : z * 8 + 16, :] = pair.astype(BF16)
        middle = []
        for low_z in range(BAND):
            merged = tile(low_z, g, 1)
            for quarter in range(1, 4):
                merged = jnp.where(place == quarter, tile(BAND * quarter + low_z, g, 1), merged)
            middle.append(merged)
        swapped = [pltpu.roll(item, 4, 0) for item in middle]
        for c in range(C):
            rows = []
            for even in range(0, BAND, 2):
                if c == 0:
                    rows.append(jnp.where(upper, middle[even], swapped[even + 1]))
                else:
                    rows.append(jnp.where(upper, swapped[even], middle[even + 1]))
            out_ref[c, g, Z * 8 :, :] = jnp.concatenate(rows, axis=0).astype(BF16)


def down_work(own, normed_ref, proj_ref, back_ref, up_ref, mine_ref, other_ref):
    total = proj_ref[...]
    total = jnp.concatenate([total[:HALF], total[HALF:] + back_ref[...]], axis=0).astype(BF16)
    lane = lax.broadcasted_iota(jnp.int32, (16, HEAD), 1)
    outs = (mine_ref, other_ref) if own == 0 else (other_ref, mine_ref)
    for z in range(0, Z, 2):
        part = dot_first(normed_ref[:, z * G * 16 : (z + 2) * G * 16], total)
        part = part.reshape(2, G, C, 8, HEAD)
        for g in range(G):
            start = g * PART + z * 8
            for c in range(C):
                down = jnp.concatenate([part[0, g, c], part[1, g, c]], axis=0)
                up = up_ref[c, g, z * 8 : z * 8 + 16, :]
                outs[c][start : start + 16, :] = jnp.where(lane < 3 * RANK, down, up.astype(F32)).astype(BF16)
    for g in range(G):
        for c in range(C):
            outs[c][g * PART + Z * 8 : (g + 1) * PART, :] = up_ref[c, g, Z * 8 :, :]


def early_down_kernel(normed_ref, proj_ref, back_ref, up_ref, mine_ref, other_ref, ready_ref):
    ready_ref[...] = jnp.zeros_like(ready_ref)

    @pl.when(lax.axis_index("c") == 0)
    def _():
        down_work(0, normed_ref, proj_ref, back_ref, up_ref, mine_ref, other_ref)


def late_down_kernel(ready_ref, normed_ref, proj_ref, back_ref, up_ref, mine_ref, other_ref):
    del ready_ref

    @pl.when(lax.axis_index("c") == 1)
    def _():
        down_work(1, normed_ref, proj_ref, back_ref, up_ref, mine_ref, other_ref)


def second_kernel(second_ref, second_come_ref, out_ref):
    @pl.when(lax.axis_index("c") == 1)
    def _():
        out_ref[...] = (second_ref[...].astype(F32) + second_come_ref[...].astype(F32)).astype(BF16)


def chip_kernel(first_ref, first_come_ref, second_ref, out_ref):
    core = lax.axis_index("c")

    @pl.when(core == 0)
    def _():
        out_ref[...] = (first_ref[...].astype(F32) + first_come_ref[...].astype(F32)).astype(BF16)

    @pl.when(core == 1)
    def _():
        out_ref[...] = second_ref[...]


def middle_kernel(come_ref, out_ref):
    total = come_ref[0].astype(F32)
    for item in range(1, G):
        total = total + come_ref[item].astype(F32)
    for z in range(Z):
        start = Z * 8 + z % BAND // 2 * 8
        tiles = jnp.concatenate([total[z * 8 : z * 8 + 8], total[start : start + 8]], axis=0)
        out_ref[z] = tiles.astype(BF16)


def last_kernel(come_ref, down_ref, up_ref):
    c, z = lax.axis_index("c"), lax.axis_index(FAR)
    total = come_ref[0].astype(F32)
    for item in range(1, Z):
        total = total + come_ref[item].astype(F32)
    total = total * ADAPTER_SCALE
    upper, lower = total[:8], total[8:]
    down_ref[...] = upper[:, : 3 * RANK].astype(BF16)
    lower = pltpu.roll(lower, (3 - z // BAND) * RANK, 1)
    moved = lax.rem(z, 2) != c
    lower = jnp.where(moved, pltpu.roll(lower, 4, 0), lower)
    both = jnp.concatenate([upper, lower], axis=0)
    both = jnp.where(c == 1, pltpu.roll(both, 4, 0), both)
    up_ref[...] = both[:12, 3 * RANK :].astype(BF16)


def shape(dims, kind=BF16):
    return jax.ShapeDtypeStruct(dims, kind)


def prepare_call(body, name, rows, extra, order, keys, values, normed, down):
    return call(
        body,
        name,
        (shape((HALF, (2 * SHIFTED + 1) * HEAD)), shape((rows, HEAD))),
        [VMEM] * len(extra) + [ANY] + [HBM] * 4,
        130_000_000,
        3_000_000,
        limit=53,
        scratch_shapes=[
            pltpu.VMEM((2, HALF, WIDTH), BF16),
            pltpu.VMEM(normed.shape, BF16),
            pltpu.VMEM(down.shape, BF16),
            pltpu.SemaphoreType.DMA((2,)),
            pltpu.SemaphoreType.DMA((2, WIDE)),
            *ORDER,
        ],
    )(*extra, order, keys, values, normed, down)


PLAIN = (shape((ROWS, 3 * NARROW)), shape((ROWS, HEAD), F32))
HALVES = (shape((HALF, 3 * NARROW)), shape((HALF, HEAD), F32))
JOINT = (shape((ROWS, 3 * NARROW)), shape((HALF, HEAD), F32), shape((HALF, HEAD)))
DSCORE = (SHIFTED, ROWS, HALF)
REST = (shape((HALF, NARROW)), shape((ROWS, HEAD), F32))


def work_call(body, name, out_shape, inputs, flops, scratch=()):
    return call(
        body,
        name,
        out_shape,
        [VMEM] * len(inputs),
        flops,
        6_000_000,
        scratch_shapes=scratch,
    )(*inputs)


PILE = shape((G * PART, HEAD))


def middle_call(come):
    return call(middle_kernel, "middle_sum", shape((Z, 16, HEAD)), [VMEM], 1_000_000, 600_000)(come)


def last_call(come):
    return call(last_kernel, "last_sum", (shape((8, 3 * RANK)), shape((12, RANK))), [VMEM], 100_000, 70_000)(come)


def per_device(normed, queries, keys, values, cotangent, down, up, order):
    normed, queries, keys, values, cotangent = (
        item[0] for item in (normed, queries, keys, values, cotangent)
    )
    ring = ("yh", "x", "c")
    count = 16
    ahead = [(item, (item + 1) % count) for item in range(count)]
    behind = [(item, (item - 1) % count) for item in range(count)]
    sources = (order, keys, values, normed, down.T)
    order = order.reshape(1, HEADS)
    inputs = (order, queries, keys, values, cotangent)
    send, tail = prepare_call(outer_kernel, "outer_parts", HALF, (), *sources)
    outer = lax.ppermute(send, ring, ahead[1::2])
    send, low = prepare_call(inner_kernel, "inner_parts", ROWS, (tail,), *sources)
    inner = lax.ppermute(send, ring, ahead[::2])
    half, half_proj, plain, plain_proj = work_call(
        own_kernel, "own_attention", HALVES + PLAIN, (*inputs, up), 2_000_000_000
    )
    late, back, far, dscore = work_call(
        joint_kernel, "joint_attention", (*JOINT, shape(DSCORE)), (*inputs, outer, up), 1_000_000_000
    )
    outer_back = lax.ppermute(back, ring, behind[::2])
    dquery, proj = work_call(
        rest_kernel, "rest_attention", REST, (order, keys, outer, up, late, dscore, plain_proj, half_proj), 500_000_000
    )
    later = work_call(
        later_kernel,
        "later_attention",
        PLAIN[:1] + JOINT + REST,
        (*inputs, inner, up, half_proj, far),
        3_000_000_000,
        [pltpu.VMEM(PLAIN[1].shape, F32), pltpu.VMEM(DSCORE, BF16)],
    )
    inner_back = lax.ppermute(later[2], ring, behind[1::2])
    up_part = work_call(
        up_kernel,
        "up_gradient",
        shape((C, G, PART, HEAD)),
        (order, plain, late, far, dquery, later[0], later[1], later[3], later[4], half, low),
        1_000_000_000,
        [pltpu.VMEM((3 * WIDTH, HEAD), F32)],
    )
    first, first_other, ready = work_call(
        early_down_kernel,
        "early_down_gradient",
        (PILE, PILE, shape((8, HEAD), F32)),
        (normed, proj, inner_back, up_part),
        500_000_000,
    )
    second_come = lax.ppermute(first_other, "c", [(0, 1)])
    second, second_other = work_call(
        late_down_kernel,
        "late_down_gradient",
        (PILE, PILE),
        (ready, normed, later[5], outer_back, up_part),
        500_000_000,
    )
    first_come = lax.ppermute(second_other, "c", [(1, 0)])
    second = work_call(second_kernel, "second_sum", PILE, (second, second_come), 1_000_000)
    chip = work_call(chip_kernel, "chip_sum", PILE, (first, first_come, second), 1_000_000)
    plane = lax.all_to_all(chip.reshape(G, PART, HEAD), NEAR, 0, 0)
    line = lax.all_to_all(middle_call(plane), FAR, 0, 0)
    down_grad, up_grad = last_call(line)
    return down_grad, up_grad.T


def solution(mesh):
    fine = Mesh(mesh.devices.reshape(16, 2, 2, 4, 2), ("z", "yl", "yh", "x", "c"))
    dp, seq = ("z", "yl"), ("yh", "x", "c")
    tokens = P(dp, seq, None)
    in_specs = (tokens,) * 5 + (P(),) * 3
    out_specs = (P(dp + seq, None), P(None, dp + seq))
    return jax.shard_map(per_device, mesh=fine, in_specs=in_specs, out_specs=out_specs, check_vma=False)
```

```python
import jax
import jax.numpy as jnp
from jax import lax
from jax.experimental import pallas as pl
from jax.experimental.pallas import tpu as pltpu
from jax.sharding import Mesh
from jax.sharding import PartitionSpec as P

HEAD = 128
ROWS = 160
HALF = 80
HEADS = 16
SHIFTED = 8
WIDTH = HEADS * HEAD
MODEL = 4096
RANK = 32
SCALE = HEAD ** -0.5
ADAPTER_SCALE = 0.25
NEAR, FAR = ("yl", "yh", "x"), ("z",)
Z, G, C = 16, 16, 2
BAND = Z // 4
WIDE = 2
NARROW = SHIFTED * HEAD
PART = Z * 8 + BAND * 4

BF16, F32 = jnp.bfloat16, jnp.float32
VMEM = pl.BlockSpec(memory_space=pltpu.VMEM)
HBM = pl.BlockSpec(memory_space=pltpu.HBM)
ANY = pl.BlockSpec(memory_space=pl.ANY)
ORDER = (pltpu.SMEM((HEADS,), jnp.int32), pltpu.SemaphoreType.DMA)


def call(body, name, out_shape, in_specs, flops, size, limit=32, out_specs=None, **rest):
    return pl.pallas_call(
        body,
        name=name,
        out_shape=out_shape,
        in_specs=in_specs,
        out_specs=out_specs or jax.tree.map(lambda _: VMEM, out_shape),
        compiler_params=pltpu.CompilerParams(vmem_limit_bytes=limit * 1024 * 1024),
        cost_estimate=pl.CostEstimate(flops=flops, bytes_accessed=size, transcendentals=0),
        **rest,
    )


def dot(left, right):
    return jnp.dot(left, right, preferred_element_type=F32)


def dot_last(left, right):
    return lax.dot_general(left, right, (((1,), (1,)), ((), ())), preferred_element_type=F32)


def dot_first(left, right):
    return lax.dot_general(left, right, (((0,), (0,)), ((), ())), preferred_element_type=F32)


def scores_of(parts, allowed):
    queries, keys, values, cotangents = zip(*parts)
    scores = [jnp.where(allowed, dot_last(key, query), -jnp.inf) for query, key in zip(queries, keys)]
    dprobs = [dot_last(value, cotangent) for value, cotangent in zip(values, cotangents)]
    tops = [jnp.max(item, axis=0, keepdims=True) for item in scores]
    powers = [jnp.exp((item - top) * SCALE) for item, top in zip(scores, tops)]
    probs = [item * (1.0 / jnp.sum(item, axis=0, keepdims=True)) for item in powers]
    weights = [item.astype(BF16) for item in probs]
    deltas = [
        jnp.sum(weight.astype(F32) * dprob, axis=0, keepdims=True) for weight, dprob in zip(weights, dprobs)
    ]
    dscores = [
        (prob * (dprob - delta)).astype(BF16) for prob, dprob, delta in zip(probs, dprobs, deltas)
    ]
    return weights, dscores


def attend(parts, allowed):
    queries, keys, _, cotangents = zip(*parts)
    weights, dscores = scores_of(parts, allowed)
    dvalues = [dot(weight, cotangent).astype(BF16) for weight, cotangent in zip(weights, cotangents)]
    dkeys = [(dot(dscore, query) * SCALE).astype(BF16) for dscore, query in zip(dscores, queries)]
    dqueries = [(dot_first(dscore, key) * SCALE).astype(BF16) for dscore, key in zip(dscores, keys)]
    return list(zip(dqueries, dkeys, dvalues))


def causal(keys, queries, ahead):
    row = lax.broadcasted_iota(jnp.int32, (keys, queries), 0)
    column = lax.broadcasted_iota(jnp.int32, (keys, queries), 1)
    return row <= column + ahead


def lanes_of(order_ref, slot, block=0):
    return pl.ds(pl.multiple_of(order_ref[slot] * HEAD + block * WIDTH, HEAD), HEAD)


def scalars(ref):
    lane = lax.broadcasted_iota(jnp.int32, (1, HEADS), 1)
    return [ref[0, slot] for slot in range(HEADS)]


def narrow_lanes(slot, block=0):
    return slice(block * NARROW + slot * HEAD, block * NARROW + (slot + 1) * HEAD)


def fetch(source_ref, order_ref, sem):
    copy = pltpu.make_async_copy(source_ref, order_ref, sem)
    copy.start()
    return copy


def start_low(normed_ref, down_ref, normed_own, down_own, wide_sems, rows):
    copies = []
    span = MODEL // WIDE
    for part in range(WIDE):
        lanes = slice(part * span, (part + 1) * span)
        copies.append(fetch(normed_ref.at[rows, lanes], normed_own.at[rows, lanes], wide_sems.at[0, part]))
        copies.append(fetch(down_ref.at[:, lanes], down_own.at[:, lanes], wide_sems.at[1, part]))
    return copies


def finish_low(copies, normed_own, down_own, rows):
    low = None
    span = MODEL // WIDE
    for part in range(WIDE):
        lanes = slice(part * span, (part + 1) * span)
        for copy in copies[2 * part : 2 * part + 2]:
            copy.wait()
        term = dot_last(normed_own[rows, lanes], down_own[:, lanes])
        low = term if low is None else low + term
    low = low.astype(BF16)
    return jnp.concatenate([low, jnp.zeros((low.shape[0], HEAD - 3 * RANK), BF16)], axis=1)


def prepare(
    rows,
    source_ref,
    key_ref,
    value_ref,
    normed_ref,
    down_ref,
    send_ref,
    low_ref,
    pair_own,
    normed_own,
    down_own,
    pair_sems,
    wide_sems,
    order_ref,
    order_sem,
):
    order_copy = fetch(source_ref, order_ref, order_sem)
    pair_copies = [
        fetch(source.at[HALF:], pair_own.at[item], pair_sems.at[item])
        for item, source in enumerate((key_ref, value_ref))
    ]
    wide_copies = start_low(normed_ref, down_ref, normed_own, down_own, wide_sems, rows)
    order_copy.wait()
    for item in range(2):
        pair_copies[item].wait()
        for slot in range(SHIFTED):
            place = item * SHIFTED + slot
            send_ref[:, place * HEAD : (place + 1) * HEAD] = pair_own[item, :, lanes_of(order_ref, slot)]
    low = finish_low(wide_copies, normed_own, down_own, rows)
    low_ref[...] = low
    send_ref[:, 2 * SHIFTED * HEAD :] = low[low.shape[0] - HALF :]


def outer_kernel(*refs):
    @pl.when(lax.axis_index("c") == 1)
    def _():
        prepare(slice(HALF, ROWS), *refs)


def inner_kernel(tail_ref, *refs):
    core = lax.axis_index("c")

    @pl.when(core == 0)
    def _():
        prepare(slice(0, ROWS), *refs)

    @pl.when(core == 1)
    def _():
        normed_ref, down_ref, low_ref = refs[3], refs[4], refs[6]
        normed_own, down_own, wide_sems = refs[8], refs[9], refs[11]
        rows = slice(0, HALF)
        copies = start_low(normed_ref, down_ref, normed_own, down_own, wide_sems, rows)
        low_ref[:HALF, :] = finish_low(copies, normed_own, down_own, rows)
        low_ref[HALF:, :] = tail_ref[...]


def project(order_ref, grads_ref, up_ref, slots, blocks=range(3), rows=slice(None)):
    total = None
    for block in blocks:
        up = jnp.concatenate([up_ref[:, lanes_of(order_ref, slot, block)] for slot in slots], axis=1)
        parts = [up if place == block else jnp.zeros_like(up) for place in range(4)]
        columns = slice(block * NARROW, (block + 1) * NARROW)
        term = dot_last(grads_ref[rows, columns], jnp.concatenate(parts, axis=0))
        total = term if total is None else total + term
    return total


def half_work(order_ref, refs, up_ref, half_ref, half_proj_ref):
    slots = range(SHIFTED)
    parts = [[ref[HALF:, lanes_of(order_ref, slot)] for ref in refs] for slot in slots]
    for slot, grads in zip(slots, attend(parts, causal(HALF, HALF, 0))):
        for block in range(3):
            half_ref[:, narrow_lanes(slot, block)] = grads[block]
    half_proj_ref[...] = project(order_ref, half_ref, up_ref, slots)


def plain_work(order_ref, refs, up_ref, plain_ref, plain_proj_ref):
    slots = range(SHIFTED, HEADS)
    parts = [[ref[:, lanes_of(order_ref, slot)] for ref in refs] for slot in slots]
    for slot, grads in zip(slots, attend(parts, causal(ROWS, ROWS, 0))):
        for block in range(3):
            plain_ref[:, narrow_lanes(slot - SHIFTED, block)] = grads[block]
    plain_proj_ref[...] = project(order_ref, plain_ref, up_ref, slots)


def joint_work(order_ref, refs, come_ref, up_ref, late_ref, back_ref, far_ref, dscore_ref):
    query_ref, key_ref, value_ref, cot_ref = refs
    far_ref[...] = come_ref[:, 2 * SHIFTED * HEAD :]
    slots = range(SHIFTED)
    parts = []
    for slot in slots:
        lanes = lanes_of(order_ref, slot)
        key, value = (
            jnp.concatenate([come_ref[:, place * HEAD : (place + 1) * HEAD], ref[:HALF, lanes]], axis=0)
            for place, ref in ((slot, key_ref), (SHIFTED + slot, value_ref))
        )
        parts.append([query_ref[:HALF, lanes], key, value, cot_ref[:HALF, lanes]])
    weights, dscores = scores_of(parts, causal(ROWS, HALF, HALF))
    for slot, (query, _, _, cotangent) in zip(slots, parts):
        dscore_ref[slot] = dscores[slot]
        for block, grad in ((1, dot(dscores[slot], query) * SCALE), (2, dot(weights[slot], cotangent))):
            grad = grad.astype(BF16)
            late_ref[:HALF, narrow_lanes(slot, block)] = grad[HALF:]
            late_ref[HALF:, narrow_lanes(slot, block)] = grad[:HALF]
    back_ref[...] = project(order_ref, late_ref, up_ref, slots, (1, 2), slice(HALF, ROWS))


def rest_work(
    order_ref, key_ref, come_ref, up_ref, late_ref, dscore_ref, plain_proj_ref, half_proj_ref, dquery_ref, proj_ref
):
    slots = range(SHIFTED)
    for slot in slots:
        far_key = come_ref[:, slot * HEAD : (slot + 1) * HEAD]
        key = jnp.concatenate([far_key, key_ref[:HALF, lanes_of(order_ref, slot)]], axis=0)
        dquery_ref[:, narrow_lanes(slot)] = (dot_first(dscore_ref[slot], key) * SCALE).astype(BF16)
    total = project(order_ref, late_ref, up_ref, slots, (1, 2), slice(0, HALF))
    total = total + project(order_ref, dquery_ref, up_ref, slots, (0,))
    plain = plain_proj_ref[...]
    proj_ref[...] = jnp.concatenate([plain[:HALF] + total, plain[HALF:] + half_proj_ref[...]], axis=0)


def own_kernel(*refs):
    source_ref, inputs, up_ref = refs[0], refs[1:5], refs[5]
    half_refs, plain_refs = refs[6:8], refs[8:10]
    order_ref = scalars(source_ref)

    @pl.when(lax.axis_index("c") == 0)
    def _():
        plain_work(order_ref, inputs, up_ref, *plain_refs)

    half_work(order_ref, inputs, up_ref, *half_refs)


def joint_kernel(*refs):
    source_ref, inputs, rest = refs[0], refs[1:5], refs[5:]

    @pl.when(lax.axis_index("c") == 0)
    def _():
        joint_work(scalars(source_ref), inputs, *rest)


def rest_kernel(source_ref, *refs):
    @pl.when(lax.axis_index("c") == 0)
    def _():
        rest_work(scalars(source_ref), *refs)


def later_kernel(*refs):
    source_ref, inputs, come_ref, up_ref, half_proj_ref = refs[0], refs[1:5], refs[5], refs[6], refs[7]
    plain_ref, late_ref, back_ref, far_ref, dquery_ref, proj_ref, plain_proj_ref, dscore_ref = refs[9:]

    @pl.when(lax.axis_index("c") == 1)
    def _():
        order_ref = scalars(source_ref)
        plain_work(order_ref, inputs, up_ref, plain_ref, plain_proj_ref)
        joint_work(order_ref, inputs, come_ref, up_ref, late_ref, back_ref, far_ref, dscore_ref)
        rest_work(
            order_ref,
            inputs[1],
            come_ref,
            up_ref,
            late_ref,
            dscore_ref,
            plain_proj_ref,
            half_proj_ref,
            dquery_ref,
            proj_ref,
        )


def accumulate(order_ref, plain_ref, late_ref, far_ref, dquery_ref, half_ref, low_ref, sums_ref):
    low = low_ref[...]
    late_low = jnp.concatenate([low, far_ref[...]], axis=0)
    rights = [
        [jnp.concatenate([item[:, block * RANK : (block + 1) * RANK]] * 4, axis=1) for block in range(3)]
        for item in (low, late_low)
    ]
    for block in range(3):
        for slot in range(SHIFTED):
            lanes = narrow_lanes(slot, block)
            sums_ref[lanes_of(order_ref, SHIFTED + slot, block), :] = dot_first(plain_ref[:, lanes], rights[0][block])
            first = late_ref[:HALF, lanes] if block else dquery_ref[:, lanes]
            left = [first, half_ref[:, lanes]] + [late_ref[HALF:, lanes]] * (block > 0)
            right = rights[1 if block else 0][block]
            sums_ref[lanes_of(order_ref, slot, block), :] = dot_first(jnp.concatenate(left, axis=0), right)


def pack(sums_ref, out_ref):
    place = lax.broadcasted_iota(jnp.int32, (8, HEAD), 1) // RANK
    upper = lax.broadcasted_iota(jnp.int32, (8, HEAD), 0) < 4

    def tile(z, g, third):
        start = ((z * G + g) * 3 + third) * 8
        return sums_ref[start : start + 8, :]

    for g in range(G):
        for z in range(0, Z, 2):
            for c in range(C):
                pair = jnp.concatenate([tile(z, g, 2 * c), tile(z + 1, g, 2 * c)], axis=0)
                out_ref[c, g, z * 8 : z * 8 + 16, :] = pair.astype(BF16)
        middle = []
        for low_z in range(BAND):
            merged = tile(low_z, g, 1)
            for quarter in range(1, 4):
                merged = jnp.where(place == quarter, tile(BAND * quarter + low_z, g, 1), merged)
            middle.append(merged)
        swapped = [pltpu.roll(item, 4, 0) for item in middle]
        for c in range(C):
            rows = []
            for even in range(0, BAND, 2):
                if c == 0:
                    rows.append(jnp.where(upper, middle[even], swapped[even + 1]))
                else:
                    rows.append(jnp.where(upper, swapped[even], middle[even + 1]))
            out_ref[c, g, Z * 8 :, :] = jnp.concatenate(rows, axis=0).astype(BF16)


def first_up_kernel(source_ref, *refs):
    out_ref, sums_ref = refs[6:]

    @pl.when(lax.axis_index("c") == 0)
    def _():
        accumulate(scalars(source_ref), *refs[:6], sums_ref)
        pack(sums_ref, out_ref)


def second_up_kernel(source_ref, back_ref, *refs):
    out_ref, back_out_ref, sums_ref = refs[6:]

    @pl.when(lax.axis_index("c") == 1)
    def _():
        accumulate(scalars(source_ref), *refs[:6], sums_ref)
        pack(sums_ref, out_ref)
        back_out_ref[...] = back_ref[...]


def down_work(own, normed_ref, proj_ref, back_ref, up_ref, mine_ref, other_ref):
    total = proj_ref[...]
    total = jnp.concatenate([total[:HALF], total[HALF:] + back_ref[...]], axis=0).astype(BF16)
    lane = lax.broadcasted_iota(jnp.int32, (16, HEAD), 1)
    outs = (mine_ref, other_ref) if own == 0 else (other_ref, mine_ref)
    for z in range(0, Z, 2):
        part = dot_first(normed_ref[:, z * G * 16 : (z + 2) * G * 16], total)
        part = part.reshape(2, G, C, 8, HEAD)
        for g in range(G):
            start = g * PART + z * 8
            for c in range(C):
                down = jnp.concatenate([part[0, g, c], part[1, g, c]], axis=0)
                up = up_ref[c, g, z * 8 : z * 8 + 16, :]
                outs[c][start : start + 16, :] = jnp.where(lane < 3 * RANK, down, up.astype(F32)).astype(BF16)
    for g in range(G):
        for c in range(C):
            outs[c][g * PART + Z * 8 : (g + 1) * PART, :] = up_ref[c, g, Z * 8 :, :]


def early_down_kernel(normed_ref, proj_ref, back_ref, up_ref, mine_ref, other_ref, ready_ref):
    ready_ref[...] = jnp.zeros_like(ready_ref)

    @pl.when(lax.axis_index("c") == 0)
    def _():
        down_work(0, normed_ref, proj_ref, back_ref, up_ref, mine_ref, other_ref)


def late_down_kernel(ready_ref, normed_ref, proj_ref, back_ref, up_ref, mine_ref, other_ref):
    del ready_ref

    @pl.when(lax.axis_index("c") == 1)
    def _():
        down_work(1, normed_ref, proj_ref, back_ref, up_ref, mine_ref, other_ref)


def second_kernel(second_ref, second_come_ref, out_ref):
    @pl.when(lax.axis_index("c") == 1)
    def _():
        out_ref[...] = (second_ref[...].astype(F32) + second_come_ref[...].astype(F32)).astype(BF16)


def chip_kernel(first_ref, first_come_ref, second_ref, out_ref):
    core = lax.axis_index("c")

    @pl.when(core == 0)
    def _():
        out_ref[...] = (first_ref[...].astype(F32) + first_come_ref[...].astype(F32)).astype(BF16)

    @pl.when(core == 1)
    def _():
        out_ref[...] = second_ref[...]


def middle_kernel(come_ref, out_ref):
    total = come_ref[0].astype(F32)
    for item in range(1, G):
        total = total + come_ref[item].astype(F32)
    for z in range(Z):
        start = Z * 8 + z % BAND // 2 * 8
        tiles = jnp.concatenate([total[z * 8 : z * 8 + 8], total[start : start + 8]], axis=0)
        out_ref[z] = tiles.astype(BF16)


def last_kernel(come_ref, down_ref, up_ref):
    c, z = lax.axis_index("c"), lax.axis_index(FAR)
    total = come_ref[0].astype(F32)
    for item in range(1, Z):
        total = total + come_ref[item].astype(F32)
    total = total * ADAPTER_SCALE
    upper, lower = total[:8], total[8:]
    down_ref[...] = upper[:, : 3 * RANK].astype(BF16)
    lower = pltpu.roll(lower, (3 - z // BAND) * RANK, 1)
    moved = lax.rem(z, 2) != c
    lower = jnp.where(moved, pltpu.roll(lower, 4, 0), lower)
    both = jnp.concatenate([upper, lower], axis=0)
    both = jnp.where(c == 1, pltpu.roll(both, 4, 0), both)
    up_ref[...] = both[:12, 3 * RANK :].astype(BF16)


def shape(dims, kind=BF16):
    return jax.ShapeDtypeStruct(dims, kind)


def prepare_call(body, name, rows, extra, order, keys, values, normed, down):
    return call(
        body,
        name,
        (shape((HALF, (2 * SHIFTED + 1) * HEAD)), shape((rows, HEAD))),
        [VMEM] * len(extra) + [ANY] + [HBM] * 4,
        130_000_000,
        3_000_000,
        limit=53,
        scratch_shapes=[
            pltpu.VMEM((2, HALF, WIDTH), BF16),
            pltpu.VMEM(normed.shape, BF16),
            pltpu.VMEM(down.shape, BF16),
            pltpu.SemaphoreType.DMA((2,)),
            pltpu.SemaphoreType.DMA((2, WIDE)),
            *ORDER,
        ],
    )(*extra, order, keys, values, normed, down)


PLAIN = (shape((ROWS, 3 * NARROW)), shape((ROWS, HEAD), F32))
HALVES = (shape((HALF, 3 * NARROW)), shape((HALF, HEAD), F32))
JOINT = (shape((ROWS, 3 * NARROW)), shape((HALF, HEAD), F32), shape((HALF, HEAD)))
DSCORE = (SHIFTED, ROWS, HALF)
REST = (shape((HALF, NARROW)), shape((ROWS, HEAD), F32))


def work_call(body, name, out_shape, inputs, flops, scratch=()):
    return call(
        body,
        name,
        out_shape,
        [VMEM] * len(inputs),
        flops,
        6_000_000,
        scratch_shapes=scratch,
    )(*inputs)


PILE = shape((G * PART, HEAD))


def middle_call(come):
    return call(middle_kernel, "middle_sum", shape((Z, 16, HEAD)), [VMEM], 1_000_000, 600_000)(come)


def last_call(come):
    return call(last_kernel, "last_sum", (shape((8, 3 * RANK)), shape((12, RANK))), [VMEM], 100_000, 70_000)(come)


def per_device(normed, queries, keys, values, cotangent, down, up, order):
    normed, queries, keys, values, cotangent = (
        item[0] for item in (normed, queries, keys, values, cotangent)
    )
    ring = ("yh", "x", "c")
    count = 16
    ahead = [(item, (item + 1) % count) for item in range(count)]
    behind = [(item, (item - 1) % count) for item in range(count)]
    sources = (order, keys, values, normed, down.T)
    order = order.reshape(1, HEADS)
    inputs = (order, queries, keys, values, cotangent)
    send, tail = prepare_call(outer_kernel, "outer_parts", HALF, (), *sources)
    outer = lax.ppermute(send, ring, ahead[1::2])
    send, low = prepare_call(inner_kernel, "inner_parts", ROWS, (tail,), *sources)
    inner = lax.ppermute(send, ring, ahead[::2])
    half, half_proj, plain, plain_proj = work_call(
        own_kernel, "own_attention", HALVES + PLAIN, (*inputs, up), 2_000_000_000
    )
    late, back, far, dscore = work_call(
        joint_kernel, "joint_attention", (*JOINT, shape(DSCORE)), (*inputs, outer, up), 1_000_000_000
    )
    outer_back = lax.ppermute(back, ring, behind[::2])
    dquery, proj = work_call(
        rest_kernel, "rest_attention", REST, (order, keys, outer, up, late, dscore, plain_proj, half_proj), 500_000_000
    )
    later = work_call(
        later_kernel,
        "later_attention",
        PLAIN[:1] + JOINT + REST,
        (*inputs, inner, up, half_proj, far),
        3_000_000_000,
        [pltpu.VMEM(PLAIN[1].shape, F32), pltpu.VMEM(DSCORE, BF16)],
    )
    sums = [pltpu.VMEM((3 * WIDTH, HEAD), F32)]
    up_shape = shape((C, G, PART, HEAD))
    second_up, inner_back = work_call(
        second_up_kernel,
        "second_up_gradient",
        (up_shape, JOINT[1]),
        (order, later[2], later[0], later[1], later[3], later[4], half, low),
        1_000_000_000,
        sums,
    )
    inner_back = lax.ppermute(inner_back, ring, behind[1::2])
    first_up = work_call(
        first_up_kernel,
        "first_up_gradient",
        up_shape,
        (order, plain, late, far, dquery, half, low),
        1_000_000_000,
        sums,
    )
    first, first_other, ready = work_call(
        early_down_kernel,
        "early_down_gradient",
        (PILE, PILE, shape((8, HEAD), F32)),
        (normed, proj, inner_back, first_up),
        500_000_000,
    )
    second_come = lax.ppermute(first_other, "c", [(0, 1)])
    second, second_other = work_call(
        late_down_kernel,
        "late_down_gradient",
        (PILE, PILE),
        (ready, normed, later[5], outer_back, second_up),
        500_000_000,
    )
    first_come = lax.ppermute(second_other, "c", [(1, 0)])
    second = work_call(second_kernel, "second_sum", PILE, (second, second_come), 1_000_000)
    chip = work_call(chip_kernel, "chip_sum", PILE, (first, first_come, second), 1_000_000)
    plane = lax.all_to_all(chip.reshape(G, PART, HEAD), NEAR, 0, 0)
    line = lax.all_to_all(middle_call(plane), FAR, 0, 0)
    down_grad, up_grad = last_call(line)
    return down_grad, up_grad.T


def solution(mesh):
    fine = Mesh(mesh.devices.reshape(16, 2, 2, 4, 2), ("z", "yl", "yh", "x", "c"))
    dp, seq = ("z", "yl"), ("yh", "x", "c")
    tokens = P(dp, seq, None)
    in_specs = (tokens,) * 5 + (P(),) * 3
    out_specs = (P(dp + seq, None), P(None, dp + seq))
    return jax.shard_map(per_device, mesh=fine, in_specs=in_specs, out_specs=out_specs, check_vma=False)
```

```python
import jax
import jax.numpy as jnp
from jax import lax
from jax.experimental import pallas as pl
from jax.experimental.pallas import tpu as pltpu
from jax.sharding import Mesh
from jax.sharding import PartitionSpec as P

HEAD = 128
ROWS = 160
HALF = 80
HEADS = 16
SHIFTED = 8
WIDTH = HEADS * HEAD
MODEL = 4096
RANK = 32
SCALE = HEAD ** -0.5
ADAPTER_SCALE = 0.25
NEAR, FAR = ("yl", "yh", "x"), ("z",)
Z, G, C = 16, 16, 2
BAND = Z // 4
WIDE = 1
NARROW = SHIFTED * HEAD
PART = Z * 8 + BAND * 4

BF16, F32 = jnp.bfloat16, jnp.float32
VMEM = pl.BlockSpec(memory_space=pltpu.VMEM)
HBM = pl.BlockSpec(memory_space=pltpu.HBM)
ANY = pl.BlockSpec(memory_space=pl.ANY)
ORDER = (pltpu.SMEM((HEADS,), jnp.int32), pltpu.SemaphoreType.DMA)


def call(body, name, out_shape, in_specs, flops, size, limit=32, out_specs=None, **rest):
    return pl.pallas_call(
        body,
        name=name,
        out_shape=out_shape,
        in_specs=in_specs,
        out_specs=out_specs or jax.tree.map(lambda _: VMEM, out_shape),
        compiler_params=pltpu.CompilerParams(vmem_limit_bytes=limit * 1024 * 1024),
        cost_estimate=pl.CostEstimate(flops=flops, bytes_accessed=size, transcendentals=0),
        **rest,
    )


def dot(left, right):
    return jnp.dot(left, right, preferred_element_type=F32)


def dot_last(left, right):
    return lax.dot_general(left, right, (((1,), (1,)), ((), ())), preferred_element_type=F32)


def dot_first(left, right):
    return lax.dot_general(left, right, (((0,), (0,)), ((), ())), preferred_element_type=F32)


def scores_of(parts, allowed):
    queries, keys, values, cotangents = zip(*parts)
    scores = [jnp.where(allowed, dot_last(key, query), -jnp.inf) for query, key in zip(queries, keys)]
    dprobs = [dot_last(value, cotangent) for value, cotangent in zip(values, cotangents)]
    tops = [jnp.max(item, axis=0, keepdims=True) for item in scores]
    powers = [jnp.exp((item - top) * SCALE) for item, top in zip(scores, tops)]
    probs = [item * (1.0 / jnp.sum(item, axis=0, keepdims=True)) for item in powers]
    weights = [item.astype(BF16) for item in probs]
    deltas = [
        jnp.sum(weight.astype(F32) * dprob, axis=0, keepdims=True) for weight, dprob in zip(weights, dprobs)
    ]
    dscores = [
        (prob * (dprob - delta)).astype(BF16) for prob, dprob, delta in zip(probs, dprobs, deltas)
    ]
    return weights, dscores


def attend(parts, allowed):
    queries, keys, _, cotangents = zip(*parts)
    weights, dscores = scores_of(parts, allowed)
    dvalues = [dot(weight, cotangent).astype(BF16) for weight, cotangent in zip(weights, cotangents)]
    dkeys = [(dot(dscore, query) * SCALE).astype(BF16) for dscore, query in zip(dscores, queries)]
    dqueries = [(dot_first(dscore, key) * SCALE).astype(BF16) for dscore, key in zip(dscores, keys)]
    return list(zip(dqueries, dkeys, dvalues))


def causal(keys, queries, ahead):
    row = lax.broadcasted_iota(jnp.int32, (keys, queries), 0)
    column = lax.broadcasted_iota(jnp.int32, (keys, queries), 1)
    return row <= column + ahead


def lanes_of(order_ref, slot, block=0):
    return pl.ds(pl.multiple_of(order_ref[slot] * HEAD + block * WIDTH, HEAD), HEAD)


def scalars(ref):
    lane = lax.broadcasted_iota(jnp.int32, (1, HEADS), 1)
    return [ref[0, slot] for slot in range(HEADS)]


def narrow_lanes(slot, block=0):
    return slice(block * NARROW + slot * HEAD, block * NARROW + (slot + 1) * HEAD)


def fetch(source_ref, order_ref, sem):
    copy = pltpu.make_async_copy(source_ref, order_ref, sem)
    copy.start()
    return copy


def start_low(normed_ref, down_ref, normed_own, down_own, wide_sems, rows):
    copies = []
    span = MODEL // WIDE
    for part in range(WIDE):
        lanes = slice(part * span, (part + 1) * span)
        copies.append(fetch(normed_ref.at[rows, lanes], normed_own.at[rows, lanes], wide_sems.at[0, part]))
        copies.append(fetch(down_ref.at[:, lanes], down_own.at[:, lanes], wide_sems.at[1, part]))
    return copies


def finish_low(copies, normed_own, down_own, rows):
    low = None
    span = MODEL // WIDE
    for part in range(WIDE):
        lanes = slice(part * span, (part + 1) * span)
        for copy in copies[2 * part : 2 * part + 2]:
            copy.wait()
        term = dot_last(normed_own[rows, lanes], down_own[:, lanes])
        low = term if low is None else low + term
    low = low.astype(BF16)
    return jnp.concatenate([low, jnp.zeros((low.shape[0], HEAD - 3 * RANK), BF16)], axis=1)


def prepare(
    rows,
    source_ref,
    key_ref,
    value_ref,
    normed_ref,
    down_ref,
    send_ref,
    low_ref,
    pair_own,
    normed_own,
    down_own,
    pair_sems,
    wide_sems,
    order_ref,
    order_sem,
):
    order_copy = fetch(source_ref, order_ref, order_sem)
    pair_copies = [
        fetch(source.at[HALF:], pair_own.at[item], pair_sems.at[item])
        for item, source in enumerate((key_ref, value_ref))
    ]
    wide_copies = start_low(normed_ref, down_ref, normed_own, down_own, wide_sems, rows)
    order_copy.wait()
    for item in range(2):
        pair_copies[item].wait()
        for slot in range(SHIFTED):
            place = item * SHIFTED + slot
            send_ref[:, place * HEAD : (place + 1) * HEAD] = pair_own[item, :, lanes_of(order_ref, slot)]
    low = finish_low(wide_copies, normed_own, down_own, rows)
    low_ref[...] = low
    send_ref[:, 2 * SHIFTED * HEAD :] = low[low.shape[0] - HALF :]


def outer_kernel(*refs):
    @pl.when(lax.axis_index("c") == 1)
    def _():
        prepare(slice(HALF, ROWS), *refs)


def inner_kernel(tail_ref, *refs):
    core = lax.axis_index("c")

    @pl.when(core == 0)
    def _():
        prepare(slice(0, ROWS), *refs)

    @pl.when(core == 1)
    def _():
        normed_ref, down_ref, low_ref = refs[3], refs[4], refs[6]
        normed_own, down_own, wide_sems = refs[8], refs[9], refs[11]
        rows = slice(0, HALF)
        copies = start_low(normed_ref, down_ref, normed_own, down_own, wide_sems, rows)
        low_ref[:HALF, :] = finish_low(copies, normed_own, down_own, rows)
        low_ref[HALF:, :] = tail_ref[...]


def project(order_ref, grads_ref, up_ref, slots, blocks=range(3), rows=slice(None)):
    total = None
    for block in blocks:
        up = jnp.concatenate([up_ref[:, lanes_of(order_ref, slot, block)] for slot in slots], axis=1)
        parts = [up if place == block else jnp.zeros_like(up) for place in range(4)]
        columns = slice(block * NARROW, (block + 1) * NARROW)
        term = dot_last(grads_ref[rows, columns], jnp.concatenate(parts, axis=0))
        total = term if total is None else total + term
    return total


def half_work(order_ref, refs, up_ref, half_ref, half_proj_ref):
    slots = range(SHIFTED)
    parts = [[ref[HALF:, lanes_of(order_ref, slot)] for ref in refs] for slot in slots]
    for slot, grads in zip(slots, attend(parts, causal(HALF, HALF, 0))):
        for block in range(3):
            half_ref[:, narrow_lanes(slot, block)] = grads[block]
    half_proj_ref[...] = project(order_ref, half_ref, up_ref, slots)


def plain_work(order_ref, refs, up_ref, plain_ref, plain_proj_ref):
    slots = range(SHIFTED, HEADS)
    parts = [[ref[:, lanes_of(order_ref, slot)] for ref in refs] for slot in slots]
    for slot, grads in zip(slots, attend(parts, causal(ROWS, ROWS, 0))):
        for block in range(3):
            plain_ref[:, narrow_lanes(slot - SHIFTED, block)] = grads[block]
    plain_proj_ref[...] = project(order_ref, plain_ref, up_ref, slots)


def joint_work(order_ref, refs, come_ref, up_ref, late_ref, back_ref, far_ref, dscore_ref):
    query_ref, key_ref, value_ref, cot_ref = refs
    far_ref[...] = come_ref[:, 2 * SHIFTED * HEAD :]
    slots = range(SHIFTED)
    parts = []
    for slot in slots:
        lanes = lanes_of(order_ref, slot)
        key, value = (
            jnp.concatenate([come_ref[:, place * HEAD : (place + 1) * HEAD], ref[:HALF, lanes]], axis=0)
            for place, ref in ((slot, key_ref), (SHIFTED + slot, value_ref))
        )
        parts.append([query_ref[:HALF, lanes], key, value, cot_ref[:HALF, lanes]])
    weights, dscores = scores_of(parts, causal(ROWS, HALF, HALF))
    for slot, (query, _, _, cotangent) in zip(slots, parts):
        dscore_ref[slot] = dscores[slot]
        for block, grad in ((1, dot(dscores[slot], query) * SCALE), (2, dot(weights[slot], cotangent))):
            grad = grad.astype(BF16)
            late_ref[:HALF, narrow_lanes(slot, block)] = grad[HALF:]
            late_ref[HALF:, narrow_lanes(slot, block)] = grad[:HALF]
    back_ref[...] = project(order_ref, late_ref, up_ref, slots, (1, 2), slice(HALF, ROWS))


def rest_work(
    order_ref, key_ref, come_ref, up_ref, late_ref, dscore_ref, plain_proj_ref, half_proj_ref, dquery_ref, proj_ref
):
    slots = range(SHIFTED)
    for slot in slots:
        far_key = come_ref[:, slot * HEAD : (slot + 1) * HEAD]
        key = jnp.concatenate([far_key, key_ref[:HALF, lanes_of(order_ref, slot)]], axis=0)
        dquery_ref[:, narrow_lanes(slot)] = (dot_first(dscore_ref[slot], key) * SCALE).astype(BF16)
    total = project(order_ref, late_ref, up_ref, slots, (1, 2), slice(0, HALF))
    total = total + project(order_ref, dquery_ref, up_ref, slots, (0,))
    plain = plain_proj_ref[...]
    proj_ref[...] = jnp.concatenate([plain[:HALF] + total, plain[HALF:] + half_proj_ref[...]], axis=0)


def own_kernel(*refs):
    source_ref, inputs, up_ref = refs[0], refs[1:5], refs[5]
    half_refs, plain_refs = refs[6:8], refs[8:10]
    order_ref = scalars(source_ref)

    @pl.when(lax.axis_index("c") == 0)
    def _():
        plain_work(order_ref, inputs, up_ref, *plain_refs)

    half_work(order_ref, inputs, up_ref, *half_refs)


def joint_kernel(*refs):
    source_ref, inputs, rest = refs[0], refs[1:5], refs[5:]

    @pl.when(lax.axis_index("c") == 0)
    def _():
        joint_work(scalars(source_ref), inputs, *rest)


def rest_kernel(source_ref, *refs):
    @pl.when(lax.axis_index("c") == 0)
    def _():
        rest_work(scalars(source_ref), *refs)


def later_kernel(*refs):
    source_ref, inputs, come_ref, up_ref, half_proj_ref = refs[0], refs[1:5], refs[5], refs[6], refs[7]
    plain_ref, late_ref, back_ref, far_ref, dquery_ref, proj_ref, plain_proj_ref, dscore_ref = refs[9:]

    @pl.when(lax.axis_index("c") == 1)
    def _():
        order_ref = scalars(source_ref)
        plain_work(order_ref, inputs, up_ref, plain_ref, plain_proj_ref)
        joint_work(order_ref, inputs, come_ref, up_ref, late_ref, back_ref, far_ref, dscore_ref)
        rest_work(
            order_ref,
            inputs[1],
            come_ref,
            up_ref,
            late_ref,
            dscore_ref,
            plain_proj_ref,
            half_proj_ref,
            dquery_ref,
            proj_ref,
        )


def accumulate(order_ref, plain_ref, late_ref, far_ref, dquery_ref, half_ref, low_ref, sums_ref):
    low = low_ref[...]
    late_low = jnp.concatenate([low, far_ref[...]], axis=0)
    rights = [
        [jnp.concatenate([item[:, block * RANK : (block + 1) * RANK]] * 4, axis=1) for block in range(3)]
        for item in (low, late_low)
    ]
    for block in range(3):
        for slot in range(SHIFTED):
            lanes = narrow_lanes(slot, block)
            sums_ref[lanes_of(order_ref, SHIFTED + slot, block), :] = dot_first(plain_ref[:, lanes], rights[0][block])
            first = late_ref[:HALF, lanes] if block else dquery_ref[:, lanes]
            left = [first, half_ref[:, lanes]] + [late_ref[HALF:, lanes]] * (block > 0)
            right = rights[1 if block else 0][block]
            sums_ref[lanes_of(order_ref, slot, block), :] = dot_first(jnp.concatenate(left, axis=0), right)


def up_kernel(*refs):
    source_ref, parts, half_ref, low_ref = refs[0], (refs[1:5], refs[5:9]), refs[9], refs[10]
    out_ref, sums_ref = refs[11:]
    order_ref = scalars(source_ref)
    for core in range(C):

        @pl.when(lax.axis_index("c") == core)
        def _():
            accumulate(order_ref, *parts[core], half_ref, low_ref, sums_ref)

    place = lax.broadcasted_iota(jnp.int32, (8, HEAD), 1) // RANK
    upper = lax.broadcasted_iota(jnp.int32, (8, HEAD), 0) < 4

    def tile(z, g, third):
        start = ((z * G + g) * 3 + third) * 8
        return sums_ref[start : start + 8, :]

    for g in range(G):
        for z in range(0, Z, 2):
            for c in range(C):
                pair = jnp.concatenate([tile(z, g, 2 * c), tile(z + 1, g, 2 * c)], axis=0)
                out_ref[c, g, z * 8 : z * 8 + 16, :] = pair.astype(BF16)
        middle = []
        for low_z in range(BAND):
            merged = tile(low_z, g, 1)
            for quarter in range(1, 4):
                merged = jnp.where(place == quarter, tile(BAND * quarter + low_z, g, 1), merged)
            middle.append(merged)
        swapped = [pltpu.roll(item, 4, 0) for item in middle]
        for c in range(C):
            rows = []
            for even in range(0, BAND, 2):
                if c == 0:
                    rows.append(jnp.where(upper, middle[even], swapped[even + 1]))
                else:
                    rows.append(jnp.where(upper, swapped[even], middle[even + 1]))
            out_ref[c, g, Z * 8 :, :] = jnp.concatenate(rows, axis=0).astype(BF16)


def down_kernel(normed_ref, first_ref, later_ref, outer_ref, inner_ref, up_ref, mine_ref, other_ref):
    own = lax.axis_index("c")
    total = jnp.where(own == 0, first_ref[...], later_ref[...])
    back = jnp.where(own == 0, inner_ref[...], outer_ref[...])
    total = jnp.concatenate([total[:HALF], total[HALF:] + back], axis=0).astype(BF16)
    lane = lax.broadcasted_iota(jnp.int32, (16, HEAD), 1)
    for z in range(0, Z, 2):
        part = dot_first(normed_ref[:, z * G * 16 : (z + 2) * G * 16], total)
        part = part.reshape(2, G, C, 8, HEAD)
        for g in range(G):
            pieces = []
            for c in range(C):
                down = jnp.concatenate([part[0, g, c], part[1, g, c]], axis=0)
                up = up_ref[c, g, z * 8 : z * 8 + 16, :]
                pieces.append(jnp.where(lane < 3 * RANK, down, up.astype(F32)).astype(BF16))
            start = g * PART + z * 8
            mine_ref[start : start + 16, :] = jnp.where(own == 0, pieces[0], pieces[1])
            other_ref[start : start + 16, :] = jnp.where(own == 0, pieces[1], pieces[0])
    for g in range(G):
        span = slice(g * PART + Z * 8, (g + 1) * PART)
        pieces = [up_ref[c, g, Z * 8 :, :] for c in range(C)]
        mine_ref[span, :] = jnp.where(own == 0, pieces[0], pieces[1])
        other_ref[span, :] = jnp.where(own == 0, pieces[1], pieces[0])


def middle_kernel(come_ref, out_ref):
    total = come_ref[0].astype(F32)
    for item in range(1, G):
        total = total + come_ref[item].astype(F32)
    for z in range(Z):
        start = Z * 8 + z % BAND // 2 * 8
        tiles = jnp.concatenate([total[z * 8 : z * 8 + 8], total[start : start + 8]], axis=0)
        out_ref[z] = tiles.astype(BF16)


def last_kernel(come_ref, down_ref, up_ref):
    c, z = lax.axis_index("c"), lax.axis_index(FAR)
    total = come_ref[0].astype(F32)
    for item in range(1, Z):
        total = total + come_ref[item].astype(F32)
    total = total * ADAPTER_SCALE
    upper, lower = total[:8], total[8:]
    down_ref[...] = upper[:, : 3 * RANK].astype(BF16)
    lower = pltpu.roll(lower, (3 - z // BAND) * RANK, 1)
    moved = lax.rem(z, 2) != c
    lower = jnp.where(moved, pltpu.roll(lower, 4, 0), lower)
    both = jnp.concatenate([upper, lower], axis=0)
    both = jnp.where(c == 1, pltpu.roll(both, 4, 0), both)
    up_ref[...] = both[:12, 3 * RANK :].astype(BF16)


def shape(dims, kind=BF16):
    return jax.ShapeDtypeStruct(dims, kind)


def prepare_call(body, name, rows, extra, order, keys, values, normed, down):
    return call(
        body,
        name,
        (shape((HALF, (2 * SHIFTED + 1) * HEAD)), shape((rows, HEAD))),
        [VMEM] * len(extra) + [ANY] + [HBM] * 4,
        130_000_000,
        3_000_000,
        limit=53,
        scratch_shapes=[
            pltpu.VMEM((2, HALF, WIDTH), BF16),
            pltpu.VMEM(normed.shape, BF16),
            pltpu.VMEM(down.shape, BF16),
            pltpu.SemaphoreType.DMA((2,)),
            pltpu.SemaphoreType.DMA((2, WIDE)),
            *ORDER,
        ],
    )(*extra, order, keys, values, normed, down)


PLAIN = (shape((ROWS, 3 * NARROW)), shape((ROWS, HEAD), F32))
HALVES = (shape((HALF, 3 * NARROW)), shape((HALF, HEAD), F32))
JOINT = (shape((ROWS, 3 * NARROW)), shape((HALF, HEAD), F32), shape((HALF, HEAD)))
DSCORE = (SHIFTED, ROWS, HALF)
REST = (shape((HALF, NARROW)), shape((ROWS, HEAD), F32))


def work_call(body, name, out_shape, inputs, flops, scratch=()):
    return call(
        body,
        name,
        out_shape,
        [VMEM] * len(inputs),
        flops,
        6_000_000,
        scratch_shapes=scratch,
    )(*inputs)


def down_call(*inputs):
    return call(
        down_kernel,
        "down_gradient",
        (shape((G * PART, HEAD)), shape((G * PART, HEAD))),
        [VMEM] * 6,
        500_000_000,
        4_000_000,
    )(*inputs)


def middle_call(come):
    return call(middle_kernel, "middle_sum", shape((Z, 16, HEAD)), [VMEM], 1_000_000, 600_000)(come)


def last_call(come):
    return call(last_kernel, "last_sum", (shape((8, 3 * RANK)), shape((12, RANK))), [VMEM], 100_000, 70_000)(come)


def per_device(normed, queries, keys, values, cotangent, down, up, order):
    normed, queries, keys, values, cotangent = (
        item[0] for item in (normed, queries, keys, values, cotangent)
    )
    ring = ("yh", "x", "c")
    count = 16
    ahead = [(item, (item + 1) % count) for item in range(count)]
    behind = [(item, (item - 1) % count) for item in range(count)]
    sources = (order, keys, values, normed, down.T)
    order = order.reshape(1, HEADS)
    inputs = (order, queries, keys, values, cotangent)
    send, tail = prepare_call(outer_kernel, "outer_parts", HALF, (), *sources)
    outer = lax.ppermute(send, ring, ahead[1::2])
    send, low = prepare_call(inner_kernel, "inner_parts", ROWS, (tail,), *sources)
    inner = lax.ppermute(send, ring, ahead[::2])
    half, half_proj, plain, plain_proj = work_call(
        own_kernel, "own_attention", HALVES + PLAIN, (*inputs, up), 2_000_000_000
    )
    late, back, far, dscore = work_call(
        joint_kernel, "joint_attention", (*JOINT, shape(DSCORE)), (*inputs, outer, up), 1_000_000_000
    )
    outer_back = lax.ppermute(back, ring, behind[::2])
    dquery, proj = work_call(
        rest_kernel, "rest_attention", REST, (order, keys, outer, up, late, dscore, plain_proj, half_proj), 500_000_000
    )
    later = work_call(
        later_kernel,
        "later_attention",
        PLAIN[:1] + JOINT + REST,
        (*inputs, inner, up, half_proj, far),
        3_000_000_000,
        [pltpu.VMEM(PLAIN[1].shape, F32), pltpu.VMEM(DSCORE, BF16)],
    )
    inner_back = lax.ppermute(later[2], ring, behind[1::2])
    up_part = work_call(
        up_kernel,
        "up_gradient",
        shape((C, G, PART, HEAD)),
        (order, plain, late, far, dquery, later[0], later[1], later[3], later[4], half, low),
        1_000_000_000,
        [pltpu.VMEM((3 * WIDTH, HEAD), F32)],
    )
    mine, other = down_call(normed, proj, later[5], outer_back, inner_back, up_part)
    other = lax.ppermute(other, "c", [(0, 1), (1, 0)])
    chip = (mine.astype(F32) + other.astype(F32)).astype(BF16)
    plane = lax.all_to_all(chip.reshape(G, PART, HEAD), NEAR, 0, 0)
    line = lax.all_to_all(middle_call(plane), FAR, 0, 0)
    down_grad, up_grad = last_call(line)
    return down_grad, up_grad.T


def solution(mesh):
    fine = Mesh(mesh.devices.reshape(16, 2, 2, 4, 2), ("z", "yl", "yh", "x", "c"))
    dp, seq = ("z", "yl"), ("yh", "x", "c")
    tokens = P(dp, seq, None)
    in_specs = (tokens,) * 5 + (P(),) * 3
    out_specs = (P(dp + seq, None), P(None, dp + seq))
    return jax.shard_map(per_device, mesh=fine, in_specs=in_specs, out_specs=out_specs, check_vma=False)
```
